32 devices in a mesh: ctx: 16 (over z, y, x), head: 2 (over core).
Axes of the slice: x: 2, y: 2, z: 4, core: 2. Of those that a mesh axis runs over, the one named last changes fastest.
Arguments:
- queries: float32 [8192, 1024], P('ctx', 'head'), may hold values from -5 to 5
- keys: float32 [8192, 1024], P('ctx', 'head'), may hold values from -5 to 5
- values: float32 [8192, 1024], P('ctx', 'head'), may hold values from -6 to 6
- transitions: float32 [8192, 1024], P('ctx', 'head'), may hold values from -6 to 6
- betas: float32 [8, 8192], P('head', 'ctx'), may hold values from 0 to 2
- documents: int32 [8192], P('ctx'), may hold values from 0 to 7, never falling along the last dimension, each value on 1 to 2048 neighbouring positions
- out_weight: float32 [1024, 2048], P('head'), may hold values from -1.5 to 1.5
Outputs:
- output: float32 [8192, 2048], P(('ctx', 'head'))
The draws below stay inside these ranges and needn't reach their ends.
Inputs may be any that keep to these rules, and one draw needn't show every extreme that they name: `documents`: document ids never fall along the tokens; every document holds at most 2048 tokens.
All inputs are finite; a program needn't handle non-finite values.
Results may differ from the reference program's by a relative error of at most 0.0003.
Values sent between devices are 32-bit elements; how exact they have to be, the bound alone decides.
No kernel may reach another device: no remote copies, remote signals or barrier semaphores. Data moves between devices by JAX's collectives and lax.ppermute only.
A program may use at most 320 MiB of HBM per device.

```python
import math
import jax
import jax.numpy as jnp
import numpy as np
from jax import lax

D = 2048
HEADS = 8
DH = 128
BLOCK_TOKENS = 512
CONTEXT_TOKENS = 8192


def paired_rows(key):
    columns = HEADS * DH
    query_rows = jax.random.truncated_normal(jax.random.fold_in(key, 101), -5.0, 5.0, (CONTEXT_TOKENS, columns))
    key_rows = jax.random.truncated_normal(jax.random.fold_in(key, 102), -5.0, 5.0, (CONTEXT_TOKENS, columns))
    return (query_rows, key_rows)


def draw_queries(key, part):
    return paired_rows(key)[0]


def draw_keys(key, part):
    return paired_rows(key)[1]


def draw_betas(key, part):
    slow_share = 0.5
    slow_heads = jax.random.uniform(jax.random.fold_in(key, 201), (HEADS, 1)) < slow_share
    small_part = jnp.exp(jax.random.uniform(jax.random.fold_in(key, 202), (HEADS, CONTEXT_TOKENS), minval=math.log(0.001), maxval=math.log(0.04)))
    apply_reflection = jax.random.uniform(jax.random.fold_in(key, 203), (HEADS, CONTEXT_TOKENS)) < 0.5
    slow_beta = jnp.where(apply_reflection, 2.0 - small_part, small_part)
    fast_beta = jax.random.uniform(jax.random.fold_in(key, 204), (HEADS, CONTEXT_TOKENS), minval=0.3, maxval=1.7)
    strengths = jnp.where(slow_heads, slow_beta, fast_beta)
    segment_count = max(CONTEXT_TOKENS // (4 * BLOCK_TOKENS), 2)
    segment_starts = jax.random.randint(jax.random.fold_in(key, 205), (segment_count,), 0, CONTEXT_TOKENS)
    block_offsets = jnp.arange(CONTEXT_TOKENS)[None, :] - segment_starts[:, None]
    inside = jnp.any((block_offsets >= 0) & (block_offsets < 40), axis=0)
    return jnp.where(inside[None, :], 1.0, strengths)


def steps_of(stream_key, shape, cuts, low, largest):
    gain, own = 1.0, jax.random.fold_in(stream_key, 6)
    for position, blocks in cuts:
        draws = jnp.exp(jax.random.uniform(jax.random.fold_in(own, position), (blocks,), jnp.float32, low / len(cuts), largest / len(cuts)))
        gain = gain * jnp.repeat(draws, shape[position] // blocks).reshape([-1 if axis == position else 1 for axis in range(len(shape))])
    return gain


def split_up(number_of, total, most, skew):
    weights = [(1 << 20) // math.isqrt(standing ** skew) + 1 for standing in range(2, number_of + 1)]
    surplus, given = total - most - (number_of - 1), [1] * (number_of - 1)
    while surplus > 0:
        free = [i for i in range(number_of - 1) if given[i] < most]
        whole, left = sum([weights[i] for i in free]), surplus
        for i in free:
            extra = min(most - given[i], max(1, left * weights[i] // whole), surplus)
            given[i] = given[i] + extra
            surplus = surplus - extra
    return np.array([most] + given)


def uneven(key, amount, total, reach, slope):
    if amount == 2:
        one = jax.random.randint(key, (), max(1, total - reach), min(reach, total - 1) + 1)
        return jnp.stack([one, total - one])
    tallies = jnp.asarray(split_up(amount, total, reach, slope), jnp.int32)
    couples = (amount - 1) // 2
    giver, sink = tallies[1:1 + 2 * couples:2], tallies[2:2 + 2 * couples:2]
    room = jnp.minimum(giver - 1, reach - sink)
    moved = jax.random.randint(jax.random.fold_in(key, 1), (couples,), 0, 1 << 20) % (room + 1)
    tallies = tallies.at[1:1 + 2 * couples:2].set(giver - moved).at[2:2 + 2 * couples:2].set(sink + moved)
    return tallies[jax.random.permutation(jax.random.fold_in(key, 2), amount)]


def gaussian(stream_key, shape, width, bound, shards=(), kind=jnp.bfloat16):
    level = steps_of(stream_key, shape, shards, -0.22, 0.18) if shards else 1.0
    result = jax.random.normal(stream_key, shape, jnp.float32) * width * level
    return jnp.minimum(jnp.maximum(result, -bound), bound).astype(kind)


def setup_inputs(seed: int = 0) -> dict:
    seeds = jax.random.split(jax.random.key(seed), 8)
    return {
        "queries": draw_queries(jax.random.fold_in(seeds[7], 71), 0),
        "keys": draw_keys(jax.random.fold_in(seeds[7], 71), 0),
        "values": gaussian(seeds[2], (CONTEXT_TOKENS, HEADS * DH), 1.0, 6.0, ((0, 16), (1, 2)), jnp.float32),
        "transitions": gaussian(seeds[3], (CONTEXT_TOKENS, HEADS * DH), 1.0, 6.0, ((0, 16), (1, 2)), jnp.float32),
        "betas": draw_betas(jax.random.fold_in(seeds[7], 71), 0),
        "documents": jnp.searchsorted(jnp.cumsum(uneven(seeds[5], CONTEXT_TOKENS // (2 * BLOCK_TOKENS), CONTEXT_TOKENS, 4 * BLOCK_TOKENS, 1)), jnp.arange(CONTEXT_TOKENS), side="right").astype(jnp.int32),
        "out_weight": gaussian(seeds[6], (HEADS * DH, D), (max(HEADS * DH // 64, 1)) ** -0.5, 1.5, ((0, 2),), jnp.float32),
    }


HIGHEST = lax.Precision.HIGHEST

def contract(pattern, left_operand, right_operand):
    return jnp.einsum(pattern, left_operand, right_operand, precision=HIGHEST)

def piece_length(length):
    return 128 if length >= 256 else length // 2

def unit_lower_inverse(lower_mat):
    lead = lower_mat.shape[:-2]
    order = lower_mat.shape[-1]
    depth = len(lead)
    inverse_blocks = jnp.ones(lead + (order, 1, 1), jnp.float32)
    size = 1
    while size < order:
        count = order // (2 * size)
        tiled = lower_mat.reshape(lead + (count, 2, size, count, 2, size))
        diagonal_tiles = jnp.diagonal(tiled, axis1=depth, axis2=depth + 3)
        lower_left = jnp.moveaxis(diagonal_tiles[..., 1, :, 0, :, :], -1, depth)
        paired = inverse_blocks.reshape(lead + (count, 2, size, size))
        upper_inverse = paired[..., 0, :, :]
        lower_inverse = paired[..., 1, :, :]
        off_block = -contract('...ij,...jk->...ik', lower_inverse, contract('...ij,...jk->...ik', lower_left, upper_inverse))
        top_half = jnp.concatenate([upper_inverse, jnp.zeros_like(upper_inverse)], axis=-1)
        bottom_half = jnp.concatenate([off_block, lower_inverse], axis=-1)
        inverse_blocks = jnp.concatenate([top_half, bottom_half], axis=-2)
        size = size * 2
    return inverse_blocks.reshape(lead + (order, order))

def local_parts(queries, keys, transitions, betas):
    batches, length, groups, head_size = queries.shape
    piece_size = piece_length(length)
    pieces = length // piece_size
    sub_shape = (batches, pieces, piece_size, groups, head_size)
    unit_dirs = transitions * lax.rsqrt(lax.optimization_barrier(jnp.sum(transitions * transitions, axis=-1, keepdims=True)) + 1e-06)
    query_sub = queries.reshape(sub_shape)
    key_sub = keys.reshape(sub_shape)
    trans_sub = unit_dirs.reshape(sub_shape)
    beta_sub = jnp.transpose(betas.reshape(batches, pieces, piece_size, groups), (0, 1, 3, 2))
    row_ids = lax.broadcasted_iota(jnp.int32, (piece_size, piece_size), 0)
    col_ids = lax.broadcasted_iota(jnp.int32, (piece_size, piece_size), 1)
    strictly = row_ids > col_ids
    within = row_ids >= col_ids
    gram_matrix = contract('bnihd,bnjhd->bnhij', trans_sub, trans_sub)
    lower_mat = jnp.eye(piece_size, dtype=jnp.float32) + jnp.where(strictly, beta_sub[..., :, None] * gram_matrix, 0.0)
    beta_keys = jnp.where(strictly, beta_sub[..., :, None] * contract('bnihd,bnjhd->bnhij', trans_sub, key_sub), 0.0)
    beta_rows = beta_sub[..., None] * jnp.transpose(trans_sub, (0, 1, 3, 2, 4))
    inverse = unit_lower_inverse(lower_mat)
    solved = contract('bnhij,bnhjk->bnhik', inverse, jnp.concatenate([beta_keys, beta_rows], axis=-1))
    carried = solved[..., :piece_size]
    applied = solved[..., piece_size:]
    query_dirs = jnp.where(within, contract('bnihd,bnshd->bnhis', query_sub, trans_sub), 0.0)
    own_scores = contract('bnihd,bnjhd->bnhij', query_sub, key_sub) - contract('bnhis,bnhsj->bnhij', query_dirs, carried)
    query_hat = jnp.transpose(query_sub, (0, 1, 3, 2, 4)) - contract('bnhis,bnhsd->bnhid', query_dirs, applied)
    key_hat = jnp.transpose(key_sub, (0, 1, 3, 2, 4)) - contract('bnhsj,bnshd->bnhjd', carried, trans_sub)
    sub_steps = jnp.eye(head_size, dtype=jnp.float32) - contract('bnshe,bnhsf->bnhef', trans_sub, applied)
    return (query_hat, key_hat, own_scores, sub_steps)

def block_form(query_hat, key_hat, own_scores, sub_steps):
    batches, pieces, groups, piece_size, head_size = query_hat.shape
    rows_out = []
    queries_out = []
    for query_index in range(pieces):
        current = query_hat[:, query_index]
        tile_list = [own_scores[:, query_index]]
        for key_index in range(query_index - 1, -1, -1):
            tile_list.insert(0, contract('bhid,bhjd->bhij', current, key_hat[:, key_index]))
            current = contract('bhie,bhef->bhif', current, sub_steps[:, key_index])
        if query_index < pieces - 1:
            tile_list.append(jnp.zeros((batches, groups, piece_size, (pieces - 1 - query_index) * piece_size), jnp.float32))
        rows_out.append(jnp.concatenate(tile_list, axis=-1))
        queries_out.append(current)
    intra_scores = jnp.concatenate(rows_out, axis=2)
    block_queries = jnp.stack(queries_out, axis=2).reshape(batches, groups, pieces * piece_size, head_size)
    suffix = jnp.broadcast_to(jnp.eye(head_size, dtype=jnp.float32), (batches, groups, head_size, head_size))
    keys_out = [None] * pieces
    for key_index in range(pieces - 1, -1, -1):
        keys_out[key_index] = contract('bhef,bhjf->bhje', suffix, key_hat[:, key_index])
        suffix = contract('bhef,bhfg->bheg', suffix, sub_steps[:, key_index])
    block_keys = jnp.stack(keys_out, axis=2).reshape(batches, groups, pieces * piece_size, head_size)
    return (block_queries, block_keys, intra_scores, suffix)

def absorb(softmax_state, raw_scores, allowed, value_part):
    row_peak, row_total, summed = softmax_state
    masked = jnp.where(allowed, raw_scores, -jnp.inf)
    new_peak = jnp.maximum(row_peak, lax.optimization_barrier(jnp.max(masked, axis=-1, keepdims=True)))
    factor = jnp.exp(row_peak - new_peak)
    weights = jnp.where(allowed, jnp.exp(masked - new_peak), 0.0)
    row_total = row_total * factor + lax.optimization_barrier(jnp.sum(weights, axis=-1, keepdims=True))
    summed = summed * factor + contract('...ij,...jd->...id', weights, value_part)
    return (new_peak, row_total, summed)

def reference(queries, keys, values, transitions, betas, documents, out_weight):
    head_count = betas.shape[0]
    head_size = queries.shape[1] // head_count
    length = BLOCK_TOKENS
    total_blocks = queries.shape[0] // length
    query_tiles = queries.reshape(total_blocks, length, head_count, head_size)
    key_blocks = keys.reshape(total_blocks, length, head_count, head_size)
    trans_blocks = transitions.reshape(total_blocks, length, head_count, head_size)
    beta_blocks = jnp.transpose(betas.reshape(head_count, total_blocks, length), (1, 2, 0))
    value_blocks = jnp.transpose(values.reshape(total_blocks, length, head_count, head_size), (0, 2, 1, 3))
    document_blocks = documents.reshape(total_blocks, length)
    score_scale = 1.0 / math.sqrt(head_size)

    def prepare(sliced):
        parts = local_parts(sliced[0][None], sliced[1][None], sliced[2][None], sliced[3][None])
        formed = block_form(*parts)
        return (formed[1][0], formed[3][0])
    all_keys, all_steps = lax.map(prepare, (query_tiles, key_blocks, trans_blocks, beta_blocks))
    causal = lax.broadcasted_iota(jnp.int32, (length, length), 0) >= lax.broadcasted_iota(jnp.int32, (length, length), 1)

    def attend(block_index):

        def pick(array):
            return lax.dynamic_index_in_dim(array, block_index, 0, keepdims=True)
        parts = local_parts(pick(query_tiles), pick(key_blocks), pick(trans_blocks), pick(beta_blocks))
        formed = block_form(*parts)
        current = formed[0][0]
        doc_row = pick(document_blocks)[0]
        own_allowed = (doc_row[:, None] == doc_row[None, :]) & causal
        softmax_state = (jnp.full((head_count, length, 1), -jnp.inf, jnp.float32), jnp.zeros((head_count, length, 1), jnp.float32), jnp.zeros((head_count, length, head_size), jnp.float32))
        softmax_state = absorb(softmax_state, formed[2][0] * score_scale, own_allowed[None], pick(value_blocks)[0])
        for distance in range(1, 4):
            source = jnp.maximum(block_index - distance, 0).astype(jnp.int32)
            if distance > 1:
                middle = jnp.maximum(block_index - distance + 1, 0).astype(jnp.int32)
                current = contract('hie,hef->hif', current, all_steps[middle])
            valid_block = block_index - distance >= 0
            allowed = (doc_row[:, None] == document_blocks[source][None, :]) & valid_block
            raw_scores = contract('hid,hjd->hij', current, all_keys[source]) * score_scale
            softmax_state = absorb(softmax_state, raw_scores, allowed[None], value_blocks[source])
        attended = softmax_state[2] / softmax_state[1]
        return jnp.transpose(attended, (1, 0, 2)).reshape(length, head_count * head_size)
    attended = lax.map(attend, jnp.arange(total_blocks, dtype=jnp.int32)).reshape(total_blocks * length, head_count * head_size)
    return jnp.dot(attended, out_weight, precision=HIGHEST, preferred_element_type=jnp.float32)
```

```python
import functools
import math

import jax
import jax.numpy as jnp
from jax import lax
from jax.experimental import pallas as pl
from jax.experimental.pallas import tpu as pltpu
from jax.sharding import PartitionSpec as P

BLOCK_TOKENS = 512
PIECE = 128
SEED = 16
BATCH = 2
ROWS = 256
GROUPS = 2
FAR = -1e30
VMEM_BYTES = 56 * 2**20
COST = 1.15e9


def lasting(microseconds):
    return pl.CostEstimate(flops=int(microseconds * COST), bytes_accessed=1000, transcendentals=0)


def split(value):
    high = value.astype(jnp.bfloat16)
    return high, (value - high.astype(jnp.float32)).astype(jnp.bfloat16)


def product(left, right, left_dim, right_dim):
    left_high, left_low = split(left)
    right_high, right_low = split(right)
    return lax.dot_general(
        jnp.concatenate([left_high, left_low, left_high], axis=left_dim),
        jnp.concatenate([right_high, right_high, right_low], axis=right_dim),
        (((left_dim,), (right_dim,)), ((), ())),
        preferred_element_type=jnp.float32,
    )


def mm(left, right):
    return product(left, right, 1, 0)


def mm_nt(left, right):
    return product(left, right, 1, 1)


def mm_tn(left, right):
    return product(left, right, 0, 0)


def columns_of(row):
    parts = [
        jnp.broadcast_to(row[:, i : i + PIECE], (PIECE, PIECE)).T
        for i in range(0, row.shape[1], PIECE)
    ]
    return jnp.concatenate(parts, axis=0) if len(parts) > 1 else parts[0]


def unit_lower_inverses(stricts):
    order = stricts[0].shape[0]
    blocks = order // SEED
    rows = lax.broadcasted_iota(jnp.int32, (order, order), 0)
    cols = lax.broadcasted_iota(jnp.int32, (order, order), 1)
    diagonal = rows // SEED == cols // SEED
    packed = []
    for strict in stricts:
        kept = jnp.where(diagonal, strict, 0.0)
        total = kept[:SEED]
        for block in range(1, blocks):
            total = total + kept[block * SEED : (block + 1) * SEED]
        packed.append(total)
    packed = jnp.concatenate(packed, axis=0)
    lane = lax.broadcasted_iota(jnp.int32, packed.shape, 1)
    row = lax.broadcasted_iota(jnp.int32, packed.shape, 0)
    shape = (len(stricts), SEED, order)
    inverse = jnp.where(lane % SEED == row % SEED, 1.0, 0.0).reshape(shape)
    first = lane - lane % SEED
    for k in range(SEED - 1):
        column = jnp.take_along_axis(packed, first + k, axis=1, mode="promise_in_bounds")
        inverse = inverse - column.reshape(shape) * inverse[:, k : k + 1, :]
    inverses = [
        jnp.where(diagonal, jnp.concatenate([inverse[i]] * blocks, axis=0), 0.0)
        for i in range(len(stricts))
    ]
    size = SEED
    while size < order:
        below = (rows // size == cols // size + 1) & (rows // (2 * size) == cols // (2 * size))
        right = [mm(jnp.where(below, s, 0.0), x) for s, x in zip(stricts, inverses)]
        inverses = [x - mm(x, r) for x, r in zip(inverses, right)]
        size *= 2
    return inverses


def stacked_values(values):
    return jnp.concatenate(split(values), axis=1)


def softmax_part(scores, stacked):
    rows, dh = scores.shape[0], stacked.shape[1] // 2
    peak = jnp.max(scores, axis=-1, keepdims=True)
    weights = jnp.exp2(scores - peak)
    total = jnp.sum(weights, axis=-1, keepdims=True)
    summed = lax.dot_general(
        jnp.concatenate(split(weights), axis=0), stacked, (((1,), (0,)), ((), ())),
        preferred_element_type=jnp.float32,
    )
    summed = summed[:rows] + summed[rows:]
    return (summed[:, :dh] + summed[:, dh:]) / total, peak + jnp.log2(total)


def stacked_keys(keys):
    high, low = split(keys)
    return jnp.concatenate([high, high, low], axis=1).T


def stacked_queries(queries):
    high, low = split(queries)
    return jnp.concatenate([high, low, high], axis=1)


def scored(queries, keys):
    return lax.dot_general(queries, keys, (((1,), (0,)), ((), ())), preferred_element_type=jnp.float32)


def prepare_kernel(q_ref, k_ref, v_ref, w_ref, beta_ref, doc_ref, qo_ref, ko_ref, st_ref, o_ref, lse_ref, *, scale):
    batch, dh, _ = st_ref.shape
    length = q_ref.shape[0]
    pieces = length // PIECE
    rows = lax.broadcasted_iota(jnp.int32, (PIECE, PIECE), 0)
    cols = lax.broadcasted_iota(jnp.int32, (PIECE, PIECE), 1)
    identity = jnp.where(rows == cols, 1.0, 0.0)
    spans = [slice(i * PIECE, (i + 1) * PIECE) for i in range(pieces)]
    heads = [slice(h * dh, (h + 1) * dh) for h in range(batch)]
    where = [(head, span) for head in heads for span in spans]
    directions = [w_ref[span, head] for head, span in where]
    units = [w * lax.rsqrt(jnp.sum(w * w, axis=-1, keepdims=True) + 1e-06) for w in directions]
    first = pl.program_id(0) * batch
    beta_rows = [beta_ref[pl.ds(first + h, 1), :] for h in range(batch)]
    betas = [columns_of(row[:, span]) for row in beta_rows for span in spans]
    grams = [
        mm_nt(jnp.concatenate([t, q_ref[span, head]], axis=0), jnp.concatenate([t, k_ref[span, head]], axis=0))
        for t, (head, span) in zip(units, where)
    ]
    inverses = unit_lower_inverses(
        [jnp.where(rows > cols, beta * g[:PIECE, :PIECE], 0.0) for beta, g in zip(betas, grams)]
    )
    solved = [
        mm(x, jnp.concatenate([jnp.where(rows > cols, beta * g[:PIECE, PIECE:], 0.0), beta * t], axis=1))
        for x, beta, g, t in zip(inverses, betas, grams, units)
    ]
    change = [mm(jnp.where(rows >= cols, g[PIECE:, :PIECE], 0.0), s) for g, s in zip(grams, solved)]
    carried = [mm_tn(s, t) for s, t in zip(solved, units)]

    def by_head(flat):
        return [flat[h * pieces : (h + 1) * pieces] for h in range(batch)]

    own = by_head([g[PIECE:, PIECE:] - c[:, :PIECE] for g, c in zip(grams, change)])
    q_hat = by_head([q_ref[span, head] - c[:, PIECE:] for (head, span), c in zip(where, change)])
    k_hat = by_head([k_ref[span, head] - c[:PIECE] for (head, span), c in zip(where, carried)])
    st = by_head([identity - c[PIECE:] for c in carried])
    tiles = [[[None] * pieces for _ in range(pieces)] for _ in range(batch)]
    for h in range(batch):
        for i in range(pieces):
            tiles[h][i][i] = own[h][i]
    current = [list(q) for q in q_hat]
    suffix = [[None] * pieces for _ in range(batch)]
    for back in range(1, pieces):
        for h in range(batch):
            for i in range(back, pieces):
                tiles[h][i][i - back] = mm_nt(current[h][i], k_hat[h][i - back])
                current[h][i] = mm_nt(current[h][i], st[h][i - back])
            j = pieces - back
            suffix[h][j - 1] = st[h][j] if back == 1 else mm(st[h][j], suffix[h][j])
    for h in range(batch):
        for i in range(pieces):
            qo_ref[h, spans[i], :] = current[h][i]
            ko_ref[h, spans[i], :] = k_hat[h][i] if i == pieces - 1 else mm(k_hat[h][i], suffix[h][i])
        st_ref[h] = mm(st[h][0], suffix[h][0]) if pieces > 1 else st[h][0]
    doc_row = (doc_ref[...].reshape(1, length) + 1).astype(jnp.float32)
    doc_col = columns_of(doc_row)
    doc_lines = [doc_row[:, span] for span in spans]
    doc_lines.append(jnp.zeros((qo_ref.shape[1] - length - pieces, dh), jnp.float32))
    doc_lines = jnp.concatenate(doc_lines, axis=0)
    for h in range(batch):
        qo_ref[h, length:, :] = doc_lines
        ko_ref[h, length:, :] = doc_lines
    stacked = [stacked_values(v_ref[:, head]) for head in heads]
    for i in range(pieces):
        for h in range(batch):
            masked = []
            for j in range(i + 1):
                same = doc_col[spans[i]] == doc_row[:, spans[j]]
                if i == j:
                    same = same & (rows >= cols)
                masked.append(jnp.where(same, tiles[h][i][j] * scale, FAR))
            out, lse = softmax_part(
                jnp.concatenate(masked, axis=1) if i else masked[0], stacked[h][: (i + 1) * PIECE]
            )
            o_ref[h, spans[i], :] = out
            lse_ref[h, spans[i], :] = jnp.broadcast_to(lse, (PIECE, PIECE))


def message_rows(length):
    return length + (length // PIECE + 7) // 8 * 8


def prepare(queries, keys, values, transitions, betas, documents, scale):
    length = queries.shape[0]
    heads = betas.shape[0]
    dh = queries.shape[1] // heads
    rows = message_rows(length)
    column = pl.BlockSpec((length, BATCH * dh), lambda h: (0, h))
    head = pl.BlockSpec((BATCH, length, dh), lambda h: (h, 0, 0))
    message = pl.BlockSpec((BATCH, rows, dh), lambda h: (h, 0, 0))
    f32 = jnp.float32
    return pl.pallas_call(
        functools.partial(prepare_kernel, scale=scale),
        grid=(heads // BATCH,),
        in_specs=[column] * 4
        + [
            pl.BlockSpec((heads, length), lambda h: (0, 0)),
            pl.BlockSpec((length,), lambda h: (0,)),
        ],
        out_specs=[message, message, pl.BlockSpec((BATCH, dh, dh), lambda h: (h, 0, 0)), head, head],
        out_shape=[
            jax.ShapeDtypeStruct((heads, rows, dh), f32),
            jax.ShapeDtypeStruct((heads, rows, dh), f32),
            jax.ShapeDtypeStruct((heads, dh, dh), f32),
            jax.ShapeDtypeStruct((heads, length, dh), f32),
            jax.ShapeDtypeStruct((heads, length, dh), f32),
        ],
        compiler_params=pltpu.CompilerParams(vmem_limit_bytes=VMEM_BYTES),
        name="prepare",
        cost_estimate=lasting(13),
    )(queries, keys, values, transitions, betas, documents)


def steps_kernel(place_ref, own_ref, near_ref, out_ref):
    even = lax.rem(place_ref[0], 2) == 0
    for h in range(own_ref.shape[0]):
        near = near_ref[h]
        out_ref[h] = jnp.where(even, near, mm(near, own_ref[h]))


def joined_steps(place, own, near):
    whole = pl.BlockSpec(own.shape, lambda i, p: (0, 0, 0))
    return pl.pallas_call(
        steps_kernel,
        grid_spec=pltpu.PrefetchScalarGridSpec(
            num_scalar_prefetch=1, grid=(1,), in_specs=[whole, whole], out_specs=whole
        ),
        out_shape=jax.ShapeDtypeStruct(own.shape, jnp.float32),
        compiler_params=pltpu.CompilerParams(vmem_limit_bytes=VMEM_BYTES),
        name="joined_steps",
        cost_estimate=lasting(2),
    )(place, own, near)


def doc_line(ref, length, valid):
    line = jnp.concatenate([ref[0, length + i : length + i + 1, :] for i in range(length // PIECE)], axis=1)
    return jnp.where(valid, line, 0.0)


def masked(scores, col, row):
    wide = jnp.concatenate([col] * (scores.shape[1] // PIECE), axis=1)
    return jnp.where(wide == row, scores, FAR)


def partner_kernel(
    place_ref, qp_ref, ko_ref, vo_ref, k1_ref, v1a_ref, v1b_ref, k2_ref, v2a_ref, v2b_ref, s_ref, u_ref, msg_ref, *, scale
):
    length = vo_ref.shape[0]
    place = place_ref[0]
    even = lax.rem(place, 2) == 0
    pick = lambda a, b: jnp.where(even, a, b)
    k1 = k1_ref[0, :length, :]
    v1 = jnp.concatenate([v1a_ref[...], v1b_ref[...]], axis=0)
    v2 = jnp.concatenate([v2a_ref[...], v2b_ref[...]], axis=0)
    near, far = place >= 2, place >= 4
    doc_1 = doc_line(k1_ref, length, near)
    docs = jnp.concatenate(
        [pick(doc_line(ko_ref, length, True), doc_1), pick(doc_1, doc_line(k2_ref, length, far))], axis=1
    )
    keys_a = stacked_keys(pick(ko_ref[0, :length, :], k1))
    keys_b = stacked_keys(mm(pick(k1, k2_ref[0, :length, :]), u_ref[0]))
    values = jnp.concatenate(
        [stacked_values(pick(vo_ref[...], v1)), stacked_values(pick(v1, v2))], axis=0
    )
    query = qp_ref[0, :length, :] * scale
    query_a = stacked_queries(query)
    query_b = stacked_queries(pick(mm_nt(query, s_ref[0]), query))
    col = columns_of(doc_line(qp_ref, length, True))
    for start in range(0, length, ROWS):
        span = slice(start, start + ROWS)
        scores = jnp.concatenate([scored(query_a[span], keys_a), scored(query_b[span], keys_b)], axis=1)
        out, lse = softmax_part(masked(scores, col[span], docs), values)
        msg_ref[0, span, :] = out
        for i in range(0, ROWS, PIECE):
            line = length + (start + i) // PIECE
            msg_ref[0, line : line + 1, :] = jnp.broadcast_to(lse[i : i + PIECE], (PIECE, PIECE)).T[:1]
    first = length + length // PIECE
    msg_ref[0, first:, :] = jnp.zeros((msg_ref.shape[1] - first, msg_ref.shape[2]), jnp.float32)


def own_kernel(place_ref, qo_ref, k1_ref, v1a_ref, v1b_ref, s_ref, u_ref, od_ref, ld_ref, out_ref, lse_ref, *, scale):
    length = od_ref.shape[1]
    place = place_ref[0]
    even = lax.rem(place, 2) == 0
    pick = lambda a, b: jnp.where(even, a, b)
    docs = doc_line(k1_ref, length, place >= 2)
    k1 = k1_ref[0, :length, :]
    keys = stacked_keys(pick(mm(k1, u_ref[0]), k1))
    values = stacked_values(jnp.concatenate([v1a_ref[...], v1b_ref[...]], axis=0))
    query = qo_ref[0, :length, :] * scale
    query = stacked_queries(pick(query, mm_nt(query, s_ref[0])))
    col = columns_of(doc_line(qo_ref, length, True))
    for start in range(0, length, ROWS):
        span = slice(start, start + ROWS)
        out, lse = softmax_part(masked(scored(query[span], keys), col[span], docs), values)
        lse_d = ld_ref[0, span, :]
        peak = jnp.maximum(lse, lse_d)
        w, w_d = jnp.exp2(lse - peak), jnp.exp2(lse_d - peak)
        total = w + w_d
        out_ref[0, span, :] = (out * w + od_ref[0, span, :] * w_d) / total
        lse_ref[0, span, :] = peak + jnp.log2(total)


def cross_specs(group, per_group, length, rows, dh):
    return {
        "all": pl.BlockSpec((1, rows, dh), lambda h, p: (group * per_group + h, 0, 0)),
        "part": pl.BlockSpec((1, rows, dh), lambda h, p: (h, 0, 0)),
        "all_values": pl.BlockSpec((length, dh), lambda h, p: (0, group * per_group + h)),
        "half_values": pl.BlockSpec((length // 2, dh), lambda h, p: (0, group * per_group + h)),
        "step": pl.BlockSpec((1, dh, dh), lambda h, p: (group * per_group + h, 0, 0)),
        "all_plain": pl.BlockSpec((1, length, dh), lambda h, p: (group * per_group + h, 0, 0)),
        "plain": pl.BlockSpec((1, length, dh), lambda h, p: (h, 0, 0)),
    }


def partner_part(group, per_group, place, q_near, k_own, values, k1, v1, k2, v2, steps, joined, scale):
    length = values.shape[0]
    _, rows, dh = q_near.shape
    spec = cross_specs(group, per_group, length, rows, dh)
    names = ["all", "all", "all_values", "part"] + ["half_values"] * 2 + ["part"] + ["half_values"] * 2 + ["step"] * 2
    return pl.pallas_call(
        functools.partial(partner_kernel, scale=scale),
        grid_spec=pltpu.PrefetchScalarGridSpec(
            num_scalar_prefetch=1,
            grid=(per_group,),
            in_specs=[spec[name] for name in names],
            out_specs=spec["part"],
        ),
        out_shape=jax.ShapeDtypeStruct((per_group, rows, dh), jnp.float32),
        compiler_params=pltpu.CompilerParams(vmem_limit_bytes=VMEM_BYTES),
        name="partner",
        cost_estimate=lasting(6),
    )(place, q_near, k_own, values, k1, *v1, k2, *v2, steps, joined)


def own_part(group, per_group, place, q_own, k1, v1, near_steps, joined, od, ld, scale):
    length = od.shape[1]
    _, rows, dh = q_own.shape
    spec = cross_specs(group, per_group, length, rows, dh)
    names = ["all", "part", "half_values", "half_values", "step", "step", "all_plain", "all_plain"]
    shape = jax.ShapeDtypeStruct((per_group, length, dh), jnp.float32)
    return pl.pallas_call(
        functools.partial(own_kernel, scale=scale),
        grid_spec=pltpu.PrefetchScalarGridSpec(
            num_scalar_prefetch=1,
            grid=(per_group,),
            in_specs=[spec[name] for name in names],
            out_specs=[spec["plain"], spec["plain"]],
        ),
        out_shape=[shape, shape],
        compiler_params=pltpu.CompilerParams(vmem_limit_bytes=VMEM_BYTES),
        name="own",
        cost_estimate=lasting(4.5),
    )(place, q_own, k1, *v1, near_steps, joined, od, ld)


def merge_kernel(core_ref, o_ref, lse_ref, msg_ref, keep_ref, send_ref):
    length, dh = o_ref.shape[1:]
    share = keep_ref.shape[0]
    parts = []
    for i in range(length // PIECE):
        span = slice(i * PIECE, (i + 1) * PIECE)
        lse = lse_ref[0, span, :]
        lse_p = columns_of(msg_ref[0, length + i : length + i + 1, :])
        peak = jnp.maximum(lse, lse_p)
        w, w_p = jnp.exp2(lse - peak), jnp.exp2(lse_p - peak)
        parts.append((o_ref[0, span, :] * w + msg_ref[0, span, :] * w_p) / (w + w_p))
    whole = jnp.concatenate(parts, axis=0)
    first = core_ref[0] == 0
    low, high = whole[:share], whole[share:]
    keep_ref[...] = jnp.where(first, low, high)
    send_ref[...] = jnp.where(first, high, low)


def merge(core, o, lse, msg):
    per_group, length, dh = o.shape
    share = length // 2
    head = pl.BlockSpec((1, length, dh), lambda h, c: (h, 0, 0))
    out = pl.BlockSpec((share, dh), lambda h, c: (0, h))
    shape = jax.ShapeDtypeStruct((share, per_group * dh), jnp.float32)
    return pl.pallas_call(
        merge_kernel,
        grid_spec=pltpu.PrefetchScalarGridSpec(
            num_scalar_prefetch=1,
            grid=(per_group,),
            in_specs=[head, head, pl.BlockSpec((1,) + msg.shape[1:], lambda h, c: (h, 0, 0))],
            out_specs=[out, out],
        ),
        out_shape=[shape, shape],
        compiler_params=pltpu.CompilerParams(vmem_limit_bytes=VMEM_BYTES),
        name="merge",
        cost_estimate=lasting(2.2),
    )(core, o, lse, msg)


def halves_kernel(own_ref, other_ref, *out_refs):
    for ref, (high, low) in zip((own_ref, other_ref), (out_refs[:2], out_refs[2:])):
        high[...], low[...] = split(ref[...])


def weight_halves(w_own, w_other):
    depth, width = w_own.shape
    tile = depth // 4
    spec = pl.BlockSpec((tile, width), lambda n: (n, 0))
    return pl.pallas_call(
        halves_kernel,
        grid=(depth // tile,),
        in_specs=[spec] * 2,
        out_specs=[spec] * 4,
        out_shape=[jax.ShapeDtypeStruct((depth, width), jnp.bfloat16)] * 4,
        compiler_params=pltpu.CompilerParams(vmem_limit_bytes=VMEM_BYTES),
        name="weight_halves",
        cost_estimate=lasting(7),
    )(w_own, w_other)


def project_kernel(*refs):
    *a_refs, own_high, own_low, other_high, other_low, out_ref = refs
    half = len(a_refs) // 2
    parts = []
    for part, high, low in ((a_refs[:half], own_high, own_low), (a_refs[half:], other_high, other_low)):
        a_high, a_low = split(jnp.concatenate([r[...] for r in part], axis=1))
        stacked = scored(jnp.concatenate([a_high, a_low], axis=0), high[...])
        rows = a_high.shape[0]
        parts.append(stacked[:rows] + (stacked[rows:] + scored(a_high, low[...])))
    out_ref[...] = parts[0] + parts[1]


def project(kept, received, weights):
    share = kept[0].shape[0]
    depth, width = weights[0].shape
    tile = min(width, 512)
    a_spec = [pl.BlockSpec(a.shape, lambda n: (0, 0)) for a in kept + received]
    w_spec = pl.BlockSpec((depth, tile), lambda n: (0, n))
    return pl.pallas_call(
        project_kernel,
        grid=(width // tile,),
        in_specs=a_spec + [w_spec] * 4,
        out_specs=pl.BlockSpec((share, tile), lambda n: (0, n)),
        out_shape=jax.ShapeDtypeStruct((share, width), jnp.float32),
        compiler_params=pltpu.CompilerParams(vmem_limit_bytes=VMEM_BYTES),
        name="project",
        cost_estimate=lasting(7.5),
    )(*kept, *received, *weights)


def onward(value, steps):
    count = lax.axis_size("ctx")
    return lax.ppermute(value, "ctx", [(i, (i + steps) % count) for i in range(count)])


def exchanged(value, axis, bit):
    return lax.ppermute(value, axis, [(i, i ^ bit) for i in range(lax.axis_size(axis))])


def after(value, *others):
    return lax.optimization_barrier((value,) + others)[0]


def shards(queries, keys, values, transitions, betas, documents, out_weight):
    heads, length = betas.shape
    dh = queries.shape[1] // heads
    assert length == BLOCK_TOKENS and lax.axis_size("ctx") % 4 == 0 and lax.axis_size("head") == 2
    per_group = heads // GROUPS
    groups = range(GROUPS)
    scale = math.log2(math.e) / math.sqrt(dh)
    index = lax.axis_index("ctx").astype(jnp.int32)
    place = index.reshape(1)
    core = lax.axis_index("head").astype(jnp.int32).reshape(1)
    far_side = lax.rem(index, 4) >= 2
    v_first, v_last = values[: length // 2], values[length // 2 :]

    def chosen(block, behind):
        return jnp.where(far_side, behind, block)

    v1_last = onward(v_last, 2)
    v2_first = onward(v_first, 4)
    w_other = exchanged(out_weight, "head", 1)
    prepared = prepare(queries, keys, values, transitions, betas, documents, scale)
    q_msg, k_msg, steps, od, ld, v2_first, w_other = lax.optimization_barrier((*prepared, v2_first, w_other))
    own_k = [k_msg[g * per_group : (g + 1) * per_group] for g in groups]
    near_steps = exchanged(steps, "ctx", 1)
    v1_first = exchanged(chosen(v_first, v2_first), "ctx", 2)
    v2_last = onward(after(v_last, steps), 4)
    k2 = [onward(own_k[0], 4)]
    q_near = exchanged(after(q_msg, near_steps), "ctx", 1)
    joined = onward(joined_steps(place, steps, near_steps), 2)
    w_other, v1_first, v1_last, v2_last = lax.optimization_barrier((w_other, v1_first, v1_last, v2_last))
    k2 += [onward(after(own_k[g], v2_last), 4) for g in groups[1:]]
    weights = weight_halves(out_weight, w_other)
    sources = [chosen(after(own_k[g], *weights), k2[g]) for g in groups]
    k1 = [exchanged(source, "ctx", 2) for source in sources]
    place = after(place, *sources)
    v1, v2 = (v1_first, v1_last), (v2_first, v2_last)
    kept, received = [], []
    for g in groups:
        msg = partner_part(g, per_group, place, q_near, k_msg, values, k1[g], v1, k2[g], v2, steps, joined, scale)
        out, lse = own_part(g, per_group, place, q_msg, k1[g], v1, near_steps, joined, od, ld, scale)
        keep, send = merge(core, out, lse, exchanged(msg, "ctx", 1))
        kept.append(keep)
        received.append(exchanged(send, "head", 1))
    return project(kept, received, weights)


def solution(mesh):
    return jax.shard_map(
        shards,
        mesh=mesh,
        in_specs=(
            P("ctx", "head"),
            P("ctx", "head"),
            P("ctx", "head"),
            P("ctx", "head"),
            P("head", "ctx"),
            P("ctx"),
            P("head", None),
        ),
        out_specs=P(("ctx", "head"), None),
        check_vma=False,
    )
```

```python
import functools
import math

import jax
import jax.numpy as jnp
from jax import lax
from jax.experimental import pallas as pl
from jax.experimental.pallas import tpu as pltpu
from jax.sharding import PartitionSpec as P

BLOCK_TOKENS = 512
PIECE = 128
SEED = 16
BATCH = 2
ROWS = 256
GROUPS = 2
FAR = -1e30
VMEM_BYTES = 56 * 2**20
COST = 1.15e9


def lasting(microseconds):
    return pl.CostEstimate(flops=int(microseconds * COST), bytes_accessed=1000, transcendentals=0)


def split(value):
    high = value.astype(jnp.bfloat16)
    return high, (value - high.astype(jnp.float32)).astype(jnp.bfloat16)


def product(left, right, left_dim, right_dim):
    left_high, left_low = split(left)
    right_high, right_low = split(right)
    return lax.dot_general(
        jnp.concatenate([left_high, left_low, left_high], axis=left_dim),
        jnp.concatenate([right_high, right_high, right_low], axis=right_dim),
        (((left_dim,), (right_dim,)), ((), ())),
        preferred_element_type=jnp.float32,
    )


def mm(left, right):
    return product(left, right, 1, 0)


def mm_nt(left, right):
    return product(left, right, 1, 1)


def mm_tn(left, right):
    return product(left, right, 0, 0)


def columns_of(row):
    parts = [
        jnp.broadcast_to(row[:, i : i + PIECE], (PIECE, PIECE)).T
        for i in range(0, row.shape[1], PIECE)
    ]
    return jnp.concatenate(parts, axis=0) if len(parts) > 1 else parts[0]


def unit_lower_inverses(stricts):
    order = stricts[0].shape[0]
    blocks = order // SEED
    rows = lax.broadcasted_iota(jnp.int32, (order, order), 0)
    cols = lax.broadcasted_iota(jnp.int32, (order, order), 1)
    diagonal = rows // SEED == cols // SEED
    packed = []
    for strict in stricts:
        kept = jnp.where(diagonal, strict, 0.0)
        total = kept[:SEED]
        for block in range(1, blocks):
            total = total + kept[block * SEED : (block + 1) * SEED]
        packed.append(total)
    packed = jnp.concatenate(packed, axis=0)
    lane = lax.broadcasted_iota(jnp.int32, packed.shape, 1)
    row = lax.broadcasted_iota(jnp.int32, packed.shape, 0)
    shape = (len(stricts), SEED, order)
    inverse = jnp.where(lane % SEED == row % SEED, 1.0, 0.0).reshape(shape)
    first = lane - lane % SEED
    for k in range(SEED - 1):
        column = jnp.take_along_axis(packed, first + k, axis=1, mode="promise_in_bounds")
        inverse = inverse - column.reshape(shape) * inverse[:, k : k + 1, :]
    inverses = [
        jnp.where(diagonal, jnp.concatenate([inverse[i]] * blocks, axis=0), 0.0)
        for i in range(len(stricts))
    ]
    size = SEED
    while size < order:
        below = (rows // size == cols // size + 1) & (rows // (2 * size) == cols // (2 * size))
        right = [mm(jnp.where(below, s, 0.0), x) for s, x in zip(stricts, inverses)]
        inverses = [x - mm(x, r) for x, r in zip(inverses, right)]
        size *= 2
    return inverses


def stacked_values(values):
    return jnp.concatenate(split(values), axis=1)


def softmax_part(scores, stacked):
    rows, dh = scores.shape[0], stacked.shape[1] // 2
    peak = jnp.max(scores, axis=-1, keepdims=True)
    weights = jnp.exp2(scores - peak)
    total = jnp.sum(weights, axis=-1, keepdims=True)
    summed = lax.dot_general(
        jnp.concatenate(split(weights), axis=0), stacked, (((1,), (0,)), ((), ())),
        preferred_element_type=jnp.float32,
    )
    summed = summed[:rows] + summed[rows:]
    return (summed[:, :dh] + summed[:, dh:]) / total, peak + jnp.log2(total)


def stacked_keys(keys):
    high, low = split(keys)
    return jnp.concatenate([high, high, low], axis=1).T


def stacked_queries(queries):
    high, low = split(queries)
    return jnp.concatenate([high, low, high], axis=1)


def scored(queries, keys):
    return lax.dot_general(queries, keys, (((1,), (0,)), ((), ())), preferred_element_type=jnp.float32)


def prepare_kernel(q_ref, k_ref, v_ref, w_ref, beta_ref, doc_ref, qo_ref, ko_ref, st_ref, o_ref, lse_ref, *, scale):
    batch, dh, _ = st_ref.shape
    length = q_ref.shape[0]
    pieces = length // PIECE
    rows = lax.broadcasted_iota(jnp.int32, (PIECE, PIECE), 0)
    cols = lax.broadcasted_iota(jnp.int32, (PIECE, PIECE), 1)
    identity = jnp.where(rows == cols, 1.0, 0.0)
    spans = [slice(i * PIECE, (i + 1) * PIECE) for i in range(pieces)]
    heads = [slice(h * dh, (h + 1) * dh) for h in range(batch)]
    where = [(head, span) for head in heads for span in spans]
    directions = [w_ref[span, head] for head, span in where]
    units = [w * lax.rsqrt(jnp.sum(w * w, axis=-1, keepdims=True) + 1e-06) for w in directions]
    first = pl.program_id(0) * batch
    beta_rows = [beta_ref[pl.ds(first + h, 1), :] for h in range(batch)]
    betas = [columns_of(row[:, span]) for row in beta_rows for span in spans]
    grams = [
        mm_nt(jnp.concatenate([t, q_ref[span, head]], axis=0), jnp.concatenate([t, k_ref[span, head]], axis=0))
        for t, (head, span) in zip(units, where)
    ]
    inverses = unit_lower_inverses(
        [jnp.where(rows > cols, beta * g[:PIECE, :PIECE], 0.0) for beta, g in zip(betas, grams)]
    )
    solved = [
        mm(x, jnp.concatenate([jnp.where(rows > cols, beta * g[:PIECE, PIECE:], 0.0), beta * t], axis=1))
        for x, beta, g, t in zip(inverses, betas, grams, units)
    ]
    change = [mm(jnp.where(rows >= cols, g[PIECE:, :PIECE], 0.0), s) for g, s in zip(grams, solved)]
    carried = [mm_tn(s, t) for s, t in zip(solved, units)]

    def by_head(flat):
        return [flat[h * pieces : (h + 1) * pieces] for h in range(batch)]

    own = by_head([g[PIECE:, PIECE:] - c[:, :PIECE] for g, c in zip(grams, change)])
    q_hat = by_head([q_ref[span, head] - c[:, PIECE:] for (head, span), c in zip(where, change)])
    k_hat = by_head([k_ref[span, head] - c[:PIECE] for (head, span), c in zip(where, carried)])
    st = by_head([identity - c[PIECE:] for c in carried])
    tiles = [[[None] * pieces for _ in range(pieces)] for _ in range(batch)]
    for h in range(batch):
        for i in range(pieces):
            tiles[h][i][i] = own[h][i]
    current = [list(q) for q in q_hat]
    suffix = [[None] * pieces for _ in range(batch)]
    for back in range(1, pieces):
        for h in range(batch):
            for i in range(back, pieces):
                tiles[h][i][i - back] = mm_nt(current[h][i], k_hat[h][i - back])
                current[h][i] = mm_nt(current[h][i], st[h][i - back])
            j = pieces - back
            suffix[h][j - 1] = st[h][j] if back == 1 else mm(st[h][j], suffix[h][j])
    for h in range(batch):
        for i in range(pieces):
            qo_ref[h, spans[i], :] = current[h][i]
            ko_ref[h, spans[i], :] = k_hat[h][i] if i == pieces - 1 else mm(k_hat[h][i], suffix[h][i])
        st_ref[h] = mm(st[h][0], suffix[h][0]) if pieces > 1 else st[h][0]
    doc_row = (doc_ref[...].reshape(1, length) + 1).astype(jnp.float32)
    doc_col = columns_of(doc_row)
    doc_lines = [doc_row[:, span] for span in spans]
    doc_lines.append(jnp.zeros((qo_ref.shape[1] - length - pieces, dh), jnp.float32))
    doc_lines = jnp.concatenate(doc_lines, axis=0)
    for h in range(batch):
        qo_ref[h, length:, :] = doc_lines
        ko_ref[h, length:, :] = doc_lines
    stacked = [stacked_values(v_ref[:, head]) for head in heads]
    for i in range(pieces):
        for h in range(batch):
            masked = []
            for j in range(i + 1):
                same = doc_col[spans[i]] == doc_row[:, spans[j]]
                if i == j:
                    same = same & (rows >= cols)
                masked.append(jnp.where(same, tiles[h][i][j] * scale, FAR))
            out, lse = softmax_part(
                jnp.concatenate(masked, axis=1) if i else masked[0], stacked[h][: (i + 1) * PIECE]
            )
            o_ref[h, spans[i], :] = out
            lse_ref[h, spans[i], :] = jnp.broadcast_to(lse, (PIECE, PIECE))


def message_rows(length):
    return length + (length // PIECE + 7) // 8 * 8


def prepare(queries, keys, values, transitions, betas, documents, scale):
    length = queries.shape[0]
    heads = betas.shape[0]
    dh = queries.shape[1] // heads
    rows = message_rows(length)
    column = pl.BlockSpec((length, BATCH * dh), lambda h: (0, h))
    head = pl.BlockSpec((BATCH, length, dh), lambda h: (h, 0, 0))
    message = pl.BlockSpec((BATCH, rows, dh), lambda h: (h, 0, 0))
    f32 = jnp.float32
    return pl.pallas_call(
        functools.partial(prepare_kernel, scale=scale),
        grid=(heads // BATCH,),
        in_specs=[column] * 4
        + [
            pl.BlockSpec((heads, length), lambda h: (0, 0)),
            pl.BlockSpec((length,), lambda h: (0,)),
        ],
        out_specs=[message, message, pl.BlockSpec((BATCH, dh, dh), lambda h: (h, 0, 0)), head, head],
        out_shape=[
            jax.ShapeDtypeStruct((heads, rows, dh), f32),
            jax.ShapeDtypeStruct((heads, rows, dh), f32),
            jax.ShapeDtypeStruct((heads, dh, dh), f32),
            jax.ShapeDtypeStruct((heads, length, dh), f32),
            jax.ShapeDtypeStruct((heads, length, dh), f32),
        ],
        compiler_params=pltpu.CompilerParams(vmem_limit_bytes=VMEM_BYTES),
        name="prepare",
        cost_estimate=lasting(13),
    )(queries, keys, values, transitions, betas, documents)


def steps_kernel(place_ref, own_ref, near_ref, out_ref):
    even = lax.rem(place_ref[0], 2) == 0
    for h in range(own_ref.shape[0]):
        near = near_ref[h]
        out_ref[h] = jnp.where(even, near, mm(near, own_ref[h]))


def joined_steps(place, own, near):
    whole = pl.BlockSpec(own.shape, lambda i, p: (0, 0, 0))
    return pl.pallas_call(
        steps_kernel,
        grid_spec=pltpu.PrefetchScalarGridSpec(
            num_scalar_prefetch=1, grid=(1,), in_specs=[whole, whole], out_specs=whole
        ),
        out_shape=jax.ShapeDtypeStruct(own.shape, jnp.float32),
        compiler_params=pltpu.CompilerParams(vmem_limit_bytes=VMEM_BYTES),
        name="joined_steps",
        cost_estimate=lasting(2),
    )(place, own, near)


def doc_line(ref, length, valid):
    line = jnp.concatenate([ref[0, length + i : length + i + 1, :] for i in range(length // PIECE)], axis=1)
    return jnp.where(valid, line, 0.0)


def masked(scores, col, row):
    wide = jnp.concatenate([col] * (scores.shape[1] // PIECE), axis=1)
    return jnp.where(wide == row, scores, FAR)


def partner_kernel(
    place_ref, qp_ref, ko_ref, vo_ref, k1_ref, v1a_ref, v1b_ref, k2_ref, v2a_ref, v2b_ref, s_ref, u_ref, msg_ref, *, scale
):
    length = vo_ref.shape[0]
    place = place_ref[0]
    even = lax.rem(place, 2) == 0
    pick = lambda a, b: jnp.where(even, a, b)
    k1 = k1_ref[0, :length, :]
    v1 = jnp.concatenate([v1a_ref[...], v1b_ref[...]], axis=0)
    v2 = jnp.concatenate([v2a_ref[...], v2b_ref[...]], axis=0)
    near, far = place >= 2, place >= 4
    doc_1 = doc_line(k1_ref, length, near)
    docs = jnp.concatenate(
        [pick(doc_line(ko_ref, length, True), doc_1), pick(doc_1, doc_line(k2_ref, length, far))], axis=1
    )
    keys_a = stacked_keys(pick(ko_ref[0, :length, :], k1))
    keys_b = stacked_keys(mm(pick(k1, k2_ref[0, :length, :]), u_ref[0]))
    values = jnp.concatenate(
        [stacked_values(pick(vo_ref[...], v1)), stacked_values(pick(v1, v2))], axis=0
    )
    query = qp_ref[0, :length, :] * scale
    query_a = stacked_queries(query)
    query_b = stacked_queries(pick(mm_nt(query, s_ref[0]), query))
    col = columns_of(doc_line(qp_ref, length, True))
    for start in range(0, length, ROWS):
        span = slice(start, start + ROWS)
        scores = jnp.concatenate([scored(query_a[span], keys_a), scored(query_b[span], keys_b)], axis=1)
        out, lse = softmax_part(masked(scores, col[span], docs), values)
        msg_ref[0, span, :] = out
        for i in range(0, ROWS, PIECE):
            line = length + (start + i) // PIECE
            msg_ref[0, line : line + 1, :] = jnp.broadcast_to(lse[i : i + PIECE], (PIECE, PIECE)).T[:1]
    first = length + length // PIECE
    msg_ref[0, first:, :] = jnp.zeros((msg_ref.shape[1] - first, msg_ref.shape[2]), jnp.float32)


def own_kernel(place_ref, qo_ref, k1_ref, v1a_ref, v1b_ref, s_ref, u_ref, od_ref, ld_ref, out_ref, lse_ref, *, scale):
    length = od_ref.shape[1]
    place = place_ref[0]
    even = lax.rem(place, 2) == 0
    pick = lambda a, b: jnp.where(even, a, b)
    docs = doc_line(k1_ref, length, place >= 2)
    k1 = k1_ref[0, :length, :]
    keys = stacked_keys(pick(mm(k1, u_ref[0]), k1))
    values = stacked_values(jnp.concatenate([v1a_ref[...], v1b_ref[...]], axis=0))
    query = qo_ref[0, :length, :] * scale
    query = stacked_queries(pick(query, mm_nt(query, s_ref[0])))
    col = columns_of(doc_line(qo_ref, length, True))
    for start in range(0, length, ROWS):
        span = slice(start, start + ROWS)
        out, lse = softmax_part(masked(scored(query[span], keys), col[span], docs), values)
        lse_d = ld_ref[0, span, :]
        peak = jnp.maximum(lse, lse_d)
        w, w_d = jnp.exp2(lse - peak), jnp.exp2(lse_d - peak)
        total = w + w_d
        out_ref[0, span, :] = (out * w + od_ref[0, span, :] * w_d) / total
        lse_ref[0, span, :] = peak + jnp.log2(total)


def cross_specs(group, per_group, length, rows, dh):
    return {
        "all": pl.BlockSpec((1, rows, dh), lambda h, p: (group * per_group + h, 0, 0)),
        "part": pl.BlockSpec((1, rows, dh), lambda h, p: (h, 0, 0)),
        "all_values": pl.BlockSpec((length, dh), lambda h, p: (0, group * per_group + h)),
        "half_values": pl.BlockSpec((length // 2, dh), lambda h, p: (0, group * per_group + h)),
        "step": pl.BlockSpec((1, dh, dh), lambda h, p: (group * per_group + h, 0, 0)),
        "all_plain": pl.BlockSpec((1, length, dh), lambda h, p: (group * per_group + h, 0, 0)),
        "plain": pl.BlockSpec((1, length, dh), lambda h, p: (h, 0, 0)),
    }


def partner_part(group, per_group, place, q_near, k_own, values, k1, v1, k2, v2, steps, joined, scale):
    length = values.shape[0]
    _, rows, dh = q_near.shape
    spec = cross_specs(group, per_group, length, rows, dh)
    names = ["all", "all", "all_values", "part"] + ["half_values"] * 2 + ["part"] + ["half_values"] * 2 + ["step"] * 2
    return pl.pallas_call(
        functools.partial(partner_kernel, scale=scale),
        grid_spec=pltpu.PrefetchScalarGridSpec(
            num_scalar_prefetch=1,
            grid=(per_group,),
            in_specs=[spec[name] for name in names],
            out_specs=spec["part"],
        ),
        out_shape=jax.ShapeDtypeStruct((per_group, rows, dh), jnp.float32),
        compiler_params=pltpu.CompilerParams(vmem_limit_bytes=VMEM_BYTES),
        name="partner",
        cost_estimate=lasting(6),
    )(place, q_near, k_own, values, k1, *v1, k2, *v2, steps, joined)


def own_part(group, per_group, place, q_own, k1, v1, near_steps, joined, od, ld, scale):
    length = od.shape[1]
    _, rows, dh = q_own.shape
    spec = cross_specs(group, per_group, length, rows, dh)
    names = ["all", "part", "half_values", "half_values", "step", "step", "all_plain", "all_plain"]
    shape = jax.ShapeDtypeStruct((per_group, length, dh), jnp.float32)
    return pl.pallas_call(
        functools.partial(own_kernel, scale=scale),
        grid_spec=pltpu.PrefetchScalarGridSpec(
            num_scalar_prefetch=1,
            grid=(per_group,),
            in_specs=[spec[name] for name in names],
            out_specs=[spec["plain"], spec["plain"]],
        ),
        out_shape=[shape, shape],
        compiler_params=pltpu.CompilerParams(vmem_limit_bytes=VMEM_BYTES),
        name="own",
        cost_estimate=lasting(4.5),
    )(place, q_own, k1, *v1, near_steps, joined, od, ld)


def merge_kernel(core_ref, o_ref, lse_ref, msg_ref, keep_ref, send_ref):
    length, dh = o_ref.shape[1:]
    share = keep_ref.shape[0]
    parts = []
    for i in range(length // PIECE):
        span = slice(i * PIECE, (i + 1) * PIECE)
        lse = lse_ref[0, span, :]
        lse_p = columns_of(msg_ref[0, length + i : length + i + 1, :])
        peak = jnp.maximum(lse, lse_p)
        w, w_p = jnp.exp2(lse - peak), jnp.exp2(lse_p - peak)
        parts.append((o_ref[0, span, :] * w + msg_ref[0, span, :] * w_p) / (w + w_p))
    whole = jnp.concatenate(parts, axis=0)
    first = core_ref[0] == 0
    low, high = whole[:share], whole[share:]
    keep_ref[...] = jnp.where(first, low, high)
    send_ref[...] = jnp.where(first, high, low)


def merge(core, o, lse, msg):
    per_group, length, dh = o.shape
    share = length // 2
    head = pl.BlockSpec((1, length, dh), lambda h, c: (h, 0, 0))
    out = pl.BlockSpec((share, dh), lambda h, c: (0, h))
    shape = jax.ShapeDtypeStruct((share, per_group * dh), jnp.float32)
    return pl.pallas_call(
        merge_kernel,
        grid_spec=pltpu.PrefetchScalarGridSpec(
            num_scalar_prefetch=1,
            grid=(per_group,),
            in_specs=[head, head, pl.BlockSpec((1,) + msg.shape[1:], lambda h, c: (h, 0, 0))],
            out_specs=[out, out],
        ),
        out_shape=[shape, shape],
        compiler_params=pltpu.CompilerParams(vmem_limit_bytes=VMEM_BYTES),
        name="merge",
        cost_estimate=lasting(2.2),
    )(core, o, lse, msg)


def halves_kernel(own_ref, other_ref, *out_refs):
    for ref, (high, low) in zip((own_ref, other_ref), (out_refs[:2], out_refs[2:])):
        high[...], low[...] = split(ref[...])


def weight_halves(w_own, w_other):
    depth, width = w_own.shape
    tile = depth // 4
    spec = pl.BlockSpec((tile, width), lambda n: (n, 0))
    return pl.pallas_call(
        halves_kernel,
        grid=(depth // tile,),
        in_specs=[spec] * 2,
        out_specs=[spec] * 4,
        out_shape=[jax.ShapeDtypeStruct((depth, width), jnp.bfloat16)] * 4,
        compiler_params=pltpu.CompilerParams(vmem_limit_bytes=VMEM_BYTES),
        name="weight_halves",
        cost_estimate=lasting(7),
    )(w_own, w_other)


def project_kernel(*refs):
    *a_refs, own_high, own_low, other_high, other_low, out_ref = refs
    half = len(a_refs) // 2
    parts = []
    for part, high, low in ((a_refs[:half], own_high, own_low), (a_refs[half:], other_high, other_low)):
        a_high, a_low = split(jnp.concatenate([r[...] for r in part], axis=1))
        stacked = scored(jnp.concatenate([a_high, a_low], axis=0), high[...])
        rows = a_high.shape[0]
        parts.append(stacked[:rows] + (stacked[rows:] + scored(a_high, low[...])))
    out_ref[...] = parts[0] + parts[1]


def project(kept, received, weights):
    share = kept[0].shape[0]
    depth, width = weights[0].shape
    tile = min(width, 512)
    a_spec = [pl.BlockSpec(a.shape, lambda n: (0, 0)) for a in kept + received]
    w_spec = pl.BlockSpec((depth, tile), lambda n: (0, n))
    return pl.pallas_call(
        project_kernel,
        grid=(width // tile,),
        in_specs=a_spec + [w_spec] * 4,
        out_specs=pl.BlockSpec((share, tile), lambda n: (0, n)),
        out_shape=jax.ShapeDtypeStruct((share, width), jnp.float32),
        compiler_params=pltpu.CompilerParams(vmem_limit_bytes=VMEM_BYTES),
        name="project",
        cost_estimate=lasting(7.5),
    )(*kept, *received, *weights)


def onward(value, steps):
    count = lax.axis_size("ctx")
    return lax.ppermute(value, "ctx", [(i, (i + steps) % count) for i in range(count)])


def exchanged(value, axis, bit):
    return lax.ppermute(value, axis, [(i, i ^ bit) for i in range(lax.axis_size(axis))])


def after(value, *others):
    return lax.optimization_barrier((value,) + others)[0]


def shards(queries, keys, values, transitions, betas, documents, out_weight):
    heads, length = betas.shape
    dh = queries.shape[1] // heads
    assert length == BLOCK_TOKENS and lax.axis_size("ctx") % 4 == 0 and lax.axis_size("head") == 2
    per_group = heads // GROUPS
    groups = range(GROUPS)
    scale = math.log2(math.e) / math.sqrt(dh)
    index = lax.axis_index("ctx").astype(jnp.int32)
    place = index.reshape(1)
    core = lax.axis_index("head").astype(jnp.int32).reshape(1)
    far_side = lax.rem(index, 4) >= 2
    v_first, v_last = values[: length // 2], values[length // 2 :]

    def chosen(block, behind):
        return jnp.where(far_side, behind, block)

    v2_first = onward(v_first, 4)
    w_other = exchanged(out_weight, "head", 1)
    prepared = prepare(queries, keys, values, transitions, betas, documents, scale)
    q_msg, k_msg, steps, od, ld, v2_first, w_other = lax.optimization_barrier((*prepared, v2_first, w_other))
    own_k = [k_msg[g * per_group : (g + 1) * per_group] for g in groups]
    near_steps = exchanged(steps, "ctx", 1)
    v1_first = exchanged(chosen(v_first, v2_first), "ctx", 2)
    v2_last = onward(after(v_last, steps), 4)
    q_near = exchanged(after(q_msg, near_steps), "ctx", 1)
    joined = joined_steps(place, steps, near_steps)
    joined = onward(joined, 2)
    source = chosen(v_last, after(v2_last, v1_first))
    v1_last = exchanged(source, "ctx", 2)
    k2 = [onward(after(block, joined, source), 4) for block in own_k]
    weights = weight_halves(out_weight, after(w_other, joined, source))
    sources = [chosen(after(own_k[g], v1_last, *weights), k2[g]) for g in groups]
    k1 = [exchanged(source, "ctx", 2) for source in sources]
    place = after(place, *sources)
    v1, v2 = (v1_first, v1_last), (v2_first, v2_last)
    kept, received = [], []
    for g in groups:
        msg = partner_part(g, per_group, place, q_near, k_msg, values, k1[g], v1, k2[g], v2, steps, joined, scale)
        out, lse = own_part(g, per_group, place, q_msg, k1[g], v1, near_steps, joined, od, ld, scale)
        keep, send = merge(core, out, lse, exchanged(msg, "ctx", 1))
        kept.append(keep)
        received.append(exchanged(send, "head", 1))
    return project(kept, received, weights)


def solution(mesh):
    return jax.shard_map(
        shards,
        mesh=mesh,
        in_specs=(
            P("ctx", "head"),
            P("ctx", "head"),
            P("ctx", "head"),
            P("ctx", "head"),
            P("head", "ctx"),
            P("ctx"),
            P("head", None),
        ),
        out_specs=P(("ctx", "head"), None),
        check_vma=False,
    )
```

```python
import functools
import math

import jax
import jax.numpy as jnp
from jax import lax
from jax.experimental import pallas as pl
from jax.experimental.pallas import tpu as pltpu
from jax.sharding import PartitionSpec as P

BLOCK_TOKENS = 512
PIECE = 128
SEED = 16
BATCH = 2
ROWS = 256
TILE = 512
GROUPS = 2
FAR = -1e30
VMEM_BYTES = 36 * 2**20
PREPARE_BYTES = 60 * 2**20
COST = 1.15e9


def lasting(microseconds):
    return pl.CostEstimate(flops=int(microseconds * COST), bytes_accessed=1000, transcendentals=0)


def split(value):
    high = value.astype(jnp.bfloat16)
    return high, (value - high.astype(jnp.float32)).astype(jnp.bfloat16)


def product(left, right, left_dim, right_dim):
    left_high, left_low = split(left)
    right_high, right_low = split(right)
    return lax.dot_general(
        jnp.concatenate([left_high, left_low, left_high], axis=left_dim),
        jnp.concatenate([right_high, right_high, right_low], axis=right_dim),
        (((left_dim,), (right_dim,)), ((), ())),
        preferred_element_type=jnp.float32,
    )


def mm(left, right):
    return product(left, right, 1, 0)


def mm_nt(left, right):
    return product(left, right, 1, 1)


def mm_tn(left, right):
    return product(left, right, 0, 0)


def columns_of(row):
    parts = [
        jnp.broadcast_to(row[:, i : i + PIECE], (PIECE, PIECE)).T
        for i in range(0, row.shape[1], PIECE)
    ]
    return jnp.concatenate(parts, axis=0) if len(parts) > 1 else parts[0]


def unit_lower_inverses(stricts):
    order = stricts[0].shape[0]
    blocks = order // SEED
    rows = lax.broadcasted_iota(jnp.int32, (order, order), 0)
    cols = lax.broadcasted_iota(jnp.int32, (order, order), 1)
    diagonal = rows // SEED == cols // SEED
    packed = []
    for strict in stricts:
        kept = jnp.where(diagonal, strict, 0.0)
        total = kept[:SEED]
        for block in range(1, blocks):
            total = total + kept[block * SEED : (block + 1) * SEED]
        packed.append(total)
    packed = jnp.concatenate(packed, axis=0)
    lane = lax.broadcasted_iota(jnp.int32, packed.shape, 1)
    row = lax.broadcasted_iota(jnp.int32, packed.shape, 0)
    shape = (len(stricts), SEED, order)
    inverse = jnp.where(lane % SEED == row % SEED, 1.0, 0.0).reshape(shape)
    first = lane - lane % SEED
    for k in range(SEED - 1):
        column = jnp.take_along_axis(packed, first + k, axis=1, mode="promise_in_bounds")
        inverse = inverse - column.reshape(shape) * inverse[:, k : k + 1, :]
    inverses = [
        jnp.where(diagonal, jnp.concatenate([inverse[i]] * blocks, axis=0), 0.0)
        for i in range(len(stricts))
    ]
    size = SEED
    while size < order:
        below = (rows // size == cols // size + 1) & (rows // (2 * size) == cols // (2 * size))
        right = [mm(jnp.where(below, s, 0.0), x) for s, x in zip(stricts, inverses)]
        inverses = [x - mm(x, r) for x, r in zip(inverses, right)]
        size *= 2
    return inverses


def stacked_values(values):
    return jnp.concatenate(split(values), axis=1)


def softmax_part(scores, stacked):
    rows, dh = scores.shape[0], stacked.shape[1] // 2
    peak = jnp.max(scores, axis=-1, keepdims=True)
    weights = jnp.exp2(scores - peak)
    total = jnp.sum(weights, axis=-1, keepdims=True)
    summed = lax.dot_general(
        jnp.concatenate(split(weights), axis=0), stacked, (((1,), (0,)), ((), ())),
        preferred_element_type=jnp.float32,
    )
    summed = summed[:rows] + summed[rows:]
    return (summed[:, :dh] + summed[:, dh:]) / total, peak + jnp.log2(total)


def stacked_keys(keys):
    high, low = split(keys)
    return jnp.concatenate([high, high, low], axis=1).T


def stacked_queries(queries):
    high, low = split(queries)
    return jnp.concatenate([high, low, high], axis=1)


def scored(queries, keys):
    return lax.dot_general(queries, keys, (((1,), (0,)), ((), ())), preferred_element_type=jnp.float32)


def prepare_kernel(q_ref, k_ref, v_ref, w_ref, beta_ref, doc_ref, qo_ref, ko_ref, st_ref, o_ref, lse_ref, *, scale):
    batch, dh, _ = st_ref.shape
    length = q_ref.shape[0]
    pieces = length // PIECE
    rows = lax.broadcasted_iota(jnp.int32, (PIECE, PIECE), 0)
    cols = lax.broadcasted_iota(jnp.int32, (PIECE, PIECE), 1)
    identity = jnp.where(rows == cols, 1.0, 0.0)
    spans = [slice(i * PIECE, (i + 1) * PIECE) for i in range(pieces)]
    heads = [slice(h * dh, (h + 1) * dh) for h in range(batch)]
    where = [(head, span) for head in heads for span in spans]
    directions = [w_ref[span, head] for head, span in where]
    units = [w * lax.rsqrt(jnp.sum(w * w, axis=-1, keepdims=True) + 1e-06) for w in directions]
    first = pl.program_id(0) * batch
    beta_rows = [beta_ref[pl.ds(first + h, 1), :] for h in range(batch)]
    betas = [columns_of(row[:, span]) for row in beta_rows for span in spans]
    grams = [
        mm_nt(jnp.concatenate([t, q_ref[span, head]], axis=0), jnp.concatenate([t, k_ref[span, head]], axis=0))
        for t, (head, span) in zip(units, where)
    ]
    inverses = unit_lower_inverses(
        [jnp.where(rows > cols, beta * g[:PIECE, :PIECE], 0.0) for beta, g in zip(betas, grams)]
    )
    solved = [
        mm(x, jnp.concatenate([jnp.where(rows > cols, beta * g[:PIECE, PIECE:], 0.0), beta * t], axis=1))
        for x, beta, g, t in zip(inverses, betas, grams, units)
    ]
    change = [mm(jnp.where(rows >= cols, g[PIECE:, :PIECE], 0.0), s) for g, s in zip(grams, solved)]
    carried = [mm_tn(s, t) for s, t in zip(solved, units)]

    def by_head(flat):
        return [flat[h * pieces : (h + 1) * pieces] for h in range(batch)]

    own = by_head([g[PIECE:, PIECE:] - c[:, :PIECE] for g, c in zip(grams, change)])
    q_hat = by_head([q_ref[span, head] - c[:, PIECE:] for (head, span), c in zip(where, change)])
    k_hat = by_head([k_ref[span, head] - c[:PIECE] for (head, span), c in zip(where, carried)])
    st = by_head([identity - c[PIECE:] for c in carried])
    tiles = [[[None] * pieces for _ in range(pieces)] for _ in range(batch)]
    for h in range(batch):
        for i in range(pieces):
            tiles[h][i][i] = own[h][i]
    current = [list(q) for q in q_hat]
    suffix = [[None] * pieces for _ in range(batch)]
    for back in range(1, pieces):
        for h in range(batch):
            for i in range(back, pieces):
                tiles[h][i][i - back] = mm_nt(current[h][i], k_hat[h][i - back])
                current[h][i] = mm_nt(current[h][i], st[h][i - back])
            j = pieces - back
            suffix[h][j - 1] = st[h][j] if back == 1 else mm(st[h][j], suffix[h][j])
    for h in range(batch):
        for i in range(pieces):
            qo_ref[h, spans[i], :] = current[h][i]
            ko_ref[h, spans[i], :] = k_hat[h][i] if i == pieces - 1 else mm(k_hat[h][i], suffix[h][i])
        st_ref[h] = mm(st[h][0], suffix[h][0]) if pieces > 1 else st[h][0]
    doc_row = (doc_ref[...].reshape(1, length) + 1).astype(jnp.float32)
    doc_col = columns_of(doc_row)
    doc_lines = [doc_row[:, span] for span in spans]
    doc_lines.append(jnp.zeros((qo_ref.shape[1] - length - pieces, dh), jnp.float32))
    doc_lines = jnp.concatenate(doc_lines, axis=0)
    for h in range(batch):
        qo_ref[h, length:, :] = doc_lines
        ko_ref[h, length:, :] = doc_lines
    stacked = [stacked_values(v_ref[:, head]) for head in heads]
    for i in range(pieces):
        for h in range(batch):
            masked = []
            for j in range(i + 1):
                same = doc_col[spans[i]] == doc_row[:, spans[j]]
                if i == j:
                    same = same & (rows >= cols)
                masked.append(jnp.where(same, tiles[h][i][j] * scale, FAR))
            out, lse = softmax_part(
                jnp.concatenate(masked, axis=1) if i else masked[0], stacked[h][: (i + 1) * PIECE]
            )
            o_ref[h, spans[i], :] = out
            lse_ref[h, spans[i], :] = jnp.broadcast_to(lse, (PIECE, PIECE))


def message_rows(length):
    return length + (length // PIECE + 7) // 8 * 8


def prepare(queries, keys, values, transitions, betas, documents, scale):
    length = queries.shape[0]
    heads = betas.shape[0]
    dh = queries.shape[1] // heads
    rows = message_rows(length)
    column = pl.BlockSpec((length, BATCH * dh), lambda h: (0, h))
    head = pl.BlockSpec((BATCH, length, dh), lambda h: (h, 0, 0))
    message = pl.BlockSpec((BATCH, rows, dh), lambda h: (h, 0, 0))
    f32 = jnp.float32
    return pl.pallas_call(
        functools.partial(prepare_kernel, scale=scale),
        grid=(heads // BATCH,),
        in_specs=[column] * 4
        + [
            pl.BlockSpec((heads, length), lambda h: (0, 0)),
            pl.BlockSpec((length,), lambda h: (0,)),
        ],
        out_specs=[message, message, pl.BlockSpec((BATCH, dh, dh), lambda h: (h, 0, 0)), head, head],
        out_shape=[
            jax.ShapeDtypeStruct((heads, rows, dh), f32),
            jax.ShapeDtypeStruct((heads, rows, dh), f32),
            jax.ShapeDtypeStruct((heads, dh, dh), f32),
            jax.ShapeDtypeStruct((heads, length, dh), f32),
            jax.ShapeDtypeStruct((heads, length, dh), f32),
        ],
        compiler_params=pltpu.CompilerParams(vmem_limit_bytes=PREPARE_BYTES),
        name="prepare",
        cost_estimate=lasting(13),
    )(queries, keys, values, transitions, betas, documents)


def steps_kernel(place_ref, own_ref, near_ref, out_ref):
    even = lax.rem(place_ref[0], 2) == 0
    for h in range(own_ref.shape[0]):
        near = near_ref[h]
        out_ref[h] = jnp.where(even, near, mm(near, own_ref[h]))


def joined_steps(place, own, near):
    whole = pl.BlockSpec(own.shape, lambda i, p: (0, 0, 0))
    return pl.pallas_call(
        steps_kernel,
        grid_spec=pltpu.PrefetchScalarGridSpec(
            num_scalar_prefetch=1, grid=(1,), in_specs=[whole, whole], out_specs=whole
        ),
        out_shape=jax.ShapeDtypeStruct(own.shape, jnp.float32),
        compiler_params=pltpu.CompilerParams(vmem_limit_bytes=VMEM_BYTES),
        name="joined_steps",
        cost_estimate=lasting(2),
    )(place, own, near)


def doc_line(ref, length, valid):
    line = jnp.concatenate([ref[0, length + i : length + i + 1, :] for i in range(length // PIECE)], axis=1)
    return jnp.where(valid, line, 0.0)


def masked(scores, col, row):
    wide = jnp.concatenate([col] * (scores.shape[1] // PIECE), axis=1)
    return jnp.where(wide == row, scores, FAR)


def attended_part(query, keys, values, docs, col):
    parts = []
    for start in range(0, query.shape[0], ROWS):
        span = slice(start, start + ROWS)
        parts.append((span, *softmax_part(masked(scored(query[span], keys), col[span], docs), values)))
    return parts


def joined_parts(out, lse, other, other_lse):
    peak = jnp.maximum(lse, other_lse)
    w, w_other = jnp.exp2(lse - peak), jnp.exp2(other_lse - peak)
    total = w + w_other
    return (out * w + other * w_other) / total, peak + jnp.log2(total)


def early_kernel(place_ref, qp_ref, ko_ref, vo_ref, k2_ref, v2a_ref, v2b_ref, u_ref, out_ref, lse_ref, *, scale):
    length, dh = vo_ref.shape
    place = place_ref[0]
    pick = lambda a, b: jnp.where(lax.rem(place, 2) == 0, a, b)
    docs = pick(doc_line(ko_ref, length, True), doc_line(k2_ref, length, place >= 4))
    keys = stacked_keys(pick(ko_ref[0, :length, :], mm(k2_ref[0, :length, :], u_ref[0])))
    values = stacked_values(
        pick(vo_ref[...], jnp.concatenate([v2a_ref[...], v2b_ref[...]], axis=0))
    )
    query = stacked_queries(qp_ref[0, :length, :] * scale)
    col = columns_of(doc_line(qp_ref, length, True))
    for span, out, lse in attended_part(query, keys, values, docs, col):
        out_ref[0, span, :] = out
        lse_ref[0, span, :] = jnp.broadcast_to(lse, (ROWS, dh))


def late_kernel(place_ref, qp_ref, k1_ref, v1a_ref, v1b_ref, s_ref, u_ref, oe_ref, le_ref, msg_ref, *, scale):
    length = oe_ref.shape[1]
    place = place_ref[0]
    pick = lambda a, b: jnp.where(lax.rem(place, 2) == 0, a, b)
    docs = doc_line(k1_ref, length, place >= 2)
    k1 = k1_ref[0, :length, :]
    keys = stacked_keys(pick(mm(k1, u_ref[0]), k1))
    values = stacked_values(jnp.concatenate([v1a_ref[...], v1b_ref[...]], axis=0))
    query = qp_ref[0, :length, :] * scale
    query = stacked_queries(pick(mm_nt(query, s_ref[0]), query))
    col = columns_of(doc_line(qp_ref, length, True))
    for span, out, lse in attended_part(query, keys, values, docs, col):
        out, lse = joined_parts(out, lse, oe_ref[0, span, :], le_ref[0, span, :])
        msg_ref[0, span, :] = out
        for i in range(0, ROWS, PIECE):
            line = length + (span.start + i) // PIECE
            msg_ref[0, line : line + 1, :] = lse[i : i + PIECE].T[:1]
    first = length + length // PIECE
    msg_ref[0, first:, :] = jnp.zeros((msg_ref.shape[1] - first, msg_ref.shape[2]), jnp.float32)


def own_kernel(place_ref, qo_ref, k1_ref, v1a_ref, v1b_ref, s_ref, u_ref, od_ref, ld_ref, out_ref, lse_ref, *, scale):
    length = od_ref.shape[1]
    place = place_ref[0]
    even = lax.rem(place, 2) == 0
    pick = lambda a, b: jnp.where(even, a, b)
    docs = doc_line(k1_ref, length, place >= 2)
    k1 = k1_ref[0, :length, :]
    keys = stacked_keys(pick(mm(k1, u_ref[0]), k1))
    values = stacked_values(jnp.concatenate([v1a_ref[...], v1b_ref[...]], axis=0))
    query = qo_ref[0, :length, :] * scale
    query = stacked_queries(pick(query, mm_nt(query, s_ref[0])))
    col = columns_of(doc_line(qo_ref, length, True))
    for span, out, lse in attended_part(query, keys, values, docs, col):
        out, lse = joined_parts(out, lse, od_ref[0, span, :], ld_ref[0, span, :])
        out_ref[0, span, :] = out
        lse_ref[0, span, :] = lse


def cross_specs(group, per_group, length, rows, dh):
    return {
        "all": pl.BlockSpec((1, rows, dh), lambda h, p: (group * per_group + h, 0, 0)),
        "part": pl.BlockSpec((1, rows, dh), lambda h, p: (h, 0, 0)),
        "all_values": pl.BlockSpec((length, dh), lambda h, p: (0, group * per_group + h)),
        "half_values": pl.BlockSpec((length // 2, dh), lambda h, p: (0, group * per_group + h)),
        "step": pl.BlockSpec((1, dh, dh), lambda h, p: (group * per_group + h, 0, 0)),
        "all_plain": pl.BlockSpec((1, length, dh), lambda h, p: (group * per_group + h, 0, 0)),
        "plain": pl.BlockSpec((1, length, dh), lambda h, p: (h, 0, 0)),
    }


def early_part(group, per_group, place, q_near, k_own, values, k2, v2, joined, scale):
    length = values.shape[0]
    _, rows, dh = q_near.shape
    spec = cross_specs(group, per_group, length, rows, dh)
    names = ["all", "all", "all_values", "part", "half_values", "half_values", "step"]
    shape = jax.ShapeDtypeStruct((per_group, length, dh), jnp.float32)
    return pl.pallas_call(
        functools.partial(early_kernel, scale=scale),
        grid_spec=pltpu.PrefetchScalarGridSpec(
            num_scalar_prefetch=1,
            grid=(per_group,),
            in_specs=[spec[name] for name in names],
            out_specs=[spec["plain"], spec["plain"]],
        ),
        out_shape=[shape, shape],
        compiler_params=pltpu.CompilerParams(vmem_limit_bytes=VMEM_BYTES),
        name="early",
        cost_estimate=lasting(4.5),
    )(place, q_near, k_own, values, k2, *v2, joined)


def late_part(group, per_group, place, q_near, k1, v1, steps, joined, early, scale):
    _, rows, dh = q_near.shape
    length = early[0].shape[1]
    spec = cross_specs(group, per_group, length, rows, dh)
    names = ["all", "part", "half_values", "half_values", "step", "step", "plain", "plain"]
    return pl.pallas_call(
        functools.partial(late_kernel, scale=scale),
        grid_spec=pltpu.PrefetchScalarGridSpec(
            num_scalar_prefetch=1,
            grid=(per_group,),
            in_specs=[spec[name] for name in names],
            out_specs=spec["part"],
        ),
        out_shape=jax.ShapeDtypeStruct((per_group, rows, dh), jnp.float32),
        compiler_params=pltpu.CompilerParams(vmem_limit_bytes=VMEM_BYTES),
        name="late",
        cost_estimate=lasting(4.5),
    )(place, q_near, k1, *v1, steps, joined, *early)


def own_part(group, per_group, place, q_own, k1, v1, near_steps, joined, od, ld, scale):
    length = od.shape[1]
    _, rows, dh = q_own.shape
    spec = cross_specs(group, per_group, length, rows, dh)
    names = ["all", "part", "half_values", "half_values", "step", "step", "all_plain", "all_plain"]
    shape = jax.ShapeDtypeStruct((per_group, length, dh), jnp.float32)
    return pl.pallas_call(
        functools.partial(own_kernel, scale=scale),
        grid_spec=pltpu.PrefetchScalarGridSpec(
            num_scalar_prefetch=1,
            grid=(per_group,),
            in_specs=[spec[name] for name in names],
            out_specs=[spec["plain"], spec["plain"]],
        ),
        out_shape=[shape, shape],
        compiler_params=pltpu.CompilerParams(vmem_limit_bytes=VMEM_BYTES),
        name="own",
        cost_estimate=lasting(4.5),
    )(place, q_own, k1, *v1, near_steps, joined, od, ld)


def merge_kernel(core_ref, o_ref, lse_ref, msg_ref, keep_ref, send_ref):
    length, dh = o_ref.shape[1:]
    share = keep_ref.shape[0]
    parts = []
    for i in range(length // PIECE):
        span = slice(i * PIECE, (i + 1) * PIECE)
        lse = lse_ref[0, span, :]
        lse_p = columns_of(msg_ref[0, length + i : length + i + 1, :])
        peak = jnp.maximum(lse, lse_p)
        w, w_p = jnp.exp2(lse - peak), jnp.exp2(lse_p - peak)
        parts.append((o_ref[0, span, :] * w + msg_ref[0, span, :] * w_p) / (w + w_p))
    whole = jnp.concatenate(parts, axis=0)
    first = core_ref[0] == 0
    low, high = whole[:share], whole[share:]
    keep_ref[...] = jnp.where(first, low, high)
    send_ref[...] = jnp.where(first, high, low)


def merge(core, o, lse, msg):
    per_group, length, dh = o.shape
    share = length // 2
    head = pl.BlockSpec((1, length, dh), lambda h, c: (h, 0, 0))
    out = pl.BlockSpec((share, dh), lambda h, c: (0, h))
    shape = jax.ShapeDtypeStruct((share, per_group * dh), jnp.float32)
    return pl.pallas_call(
        merge_kernel,
        grid_spec=pltpu.PrefetchScalarGridSpec(
            num_scalar_prefetch=1,
            grid=(per_group,),
            in_specs=[head, head, pl.BlockSpec((1,) + msg.shape[1:], lambda h, c: (h, 0, 0))],
            out_specs=[out, out],
        ),
        out_shape=[shape, shape],
        compiler_params=pltpu.CompilerParams(vmem_limit_bytes=VMEM_BYTES),
        name="merge",
        cost_estimate=lasting(2.2),
    )(core, o, lse, msg)


def halves_kernel(own_ref, other_ref, *out_refs):
    for ref, (high, low) in zip((own_ref, other_ref), (out_refs[:2], out_refs[2:])):
        high[pl.program_id(0)], low[pl.program_id(0)] = split(ref[...])


def weight_halves(w_own, w_other):
    depth, width = w_own.shape
    tile = min(width, TILE)
    spec = pl.BlockSpec((depth, tile), lambda n: (0, n))
    kept = pl.BlockSpec(memory_space=pltpu.VMEM)
    return pl.pallas_call(
        halves_kernel,
        grid=(width // tile,),
        in_specs=[spec] * 2,
        out_specs=[kept] * 4,
        out_shape=[pltpu.VMEM((width // tile, depth, tile), jnp.bfloat16)] * 4,
        compiler_params=pltpu.CompilerParams(vmem_limit_bytes=VMEM_BYTES),
        name="weight_halves",
        cost_estimate=lasting(7),
    )(w_own, w_other)


def project_kernel(*refs):
    *a_refs, own_high, own_low, other_high, other_low, out_ref = refs
    half = len(a_refs) // 2
    parts = []
    for part, high, low in ((a_refs[:half], own_high, own_low), (a_refs[half:], other_high, other_low)):
        a_high, a_low = split(jnp.concatenate([r[...] for r in part], axis=1))
        stacked = scored(jnp.concatenate([a_high, a_low], axis=0), high[pl.program_id(0)])
        rows = a_high.shape[0]
        parts.append(stacked[:rows] + (stacked[rows:] + scored(a_high, low[pl.program_id(0)])))
    out_ref[...] = parts[0] + parts[1]


def project(kept, received, weights):
    share = kept[0].shape[0]
    tiles, depth, tile = weights[0].shape
    width = tiles * tile
    a_spec = [pl.BlockSpec(a.shape, lambda n: (0, 0)) for a in kept + received]
    w_spec = pl.BlockSpec(memory_space=pltpu.VMEM)
    return pl.pallas_call(
        project_kernel,
        grid=(tiles,),
        in_specs=a_spec + [w_spec] * 4,
        out_specs=pl.BlockSpec((share, tile), lambda n: (0, n)),
        out_shape=jax.ShapeDtypeStruct((share, width), jnp.float32),
        compiler_params=pltpu.CompilerParams(vmem_limit_bytes=VMEM_BYTES),
        name="project",
        cost_estimate=lasting(7.5),
    )(*kept, *received, *weights)


def onward(value, steps):
    count = lax.axis_size("ctx")
    return lax.ppermute(value, "ctx", [(i, (i + steps) % count) for i in range(count)])


def exchanged(value, axis, bit):
    return lax.ppermute(value, axis, [(i, i ^ bit) for i in range(lax.axis_size(axis))])


def after(value, *others):
    return lax.optimization_barrier((value,) + others)[0]


def shards(queries, keys, values, transitions, betas, documents, out_weight):
    heads, length = betas.shape
    dh = queries.shape[1] // heads
    assert length == BLOCK_TOKENS and lax.axis_size("ctx") % 4 == 0 and lax.axis_size("head") == 2
    per_group = heads // GROUPS
    groups = range(GROUPS)
    scale = math.log2(math.e) / math.sqrt(dh)
    index = lax.axis_index("ctx").astype(jnp.int32)
    place = index.reshape(1)
    core = lax.axis_index("head").astype(jnp.int32).reshape(1)
    far_side = lax.rem(index, 4) >= 2
    v_first, v_last = values[: length // 2], values[length // 2 :]

    def chosen(block, behind):
        return jnp.where(far_side, behind, block)

    v2_first = onward(v_first, 4)
    w_other = exchanged(out_weight, "head", 1)
    prepared = prepare(queries, keys, values, transitions, betas, documents, scale)
    q_msg, k_msg, steps, od, ld, v2_first, w_other = lax.optimization_barrier((*prepared, v2_first, w_other))
    own_k = [k_msg[g * per_group : (g + 1) * per_group] for g in groups]
    near_steps = exchanged(steps, "ctx", 1)
    v1_first = exchanged(chosen(v_first, v2_first), "ctx", 2)
    v2_last = onward(after(v_last, steps), 4)
    q_near = exchanged(after(q_msg, near_steps), "ctx", 1)
    joined = joined_steps(place, steps, near_steps)
    joined = onward(joined, 2)
    source = chosen(v_last, after(v2_last, v1_first))
    v1_last = exchanged(source, "ctx", 2)
    k2 = [onward(after(block, joined, source), 4) for block in own_k]
    weights = weight_halves(out_weight, after(w_other, joined, source))
    sources = [chosen(after(own_k[0], v1_last), k2[0])]
    v1, v2 = (v1_first, v1_last), (v2_first, v2_last)
    early = []
    for g in groups:
        if g:
            sources.append(chosen(after(own_k[g], early[-1][0]), k2[g]))
        ready = after(place, sources[g], *weights)
        early.append(early_part(g, per_group, ready, q_near, k_msg, values, k2[g], v2, joined, scale))
    k1 = [exchanged(source, "ctx", 2) for source in sources]
    kept, received = [], []
    for g in groups:
        msg = late_part(g, per_group, place, q_near, k1[g], v1, steps, joined, early[g], scale)
        out, lse = own_part(g, per_group, place, q_msg, k1[g], v1, near_steps, joined, od, ld, scale)
        keep, send = merge(core, out, lse, exchanged(msg, "ctx", 1))
        kept.append(keep)
        received.append(exchanged(send, "head", 1))
    return project(kept, received, weights)


def solution(mesh):
    return jax.shard_map(
        shards,
        mesh=mesh,
        in_specs=(
            P("ctx", "head"),
            P("ctx", "head"),
            P("ctx", "head"),
            P("ctx", "head"),
            P("head", "ctx"),
            P("ctx"),
            P("head", None),
        ),
        out_specs=P(("ctx", "head"), None),
        check_vma=False,
    )
```

```python
import functools
import math

import jax
import jax.numpy as jnp
from jax import lax
from jax.experimental import pallas as pl
from jax.experimental.pallas import tpu as pltpu
from jax.sharding import PartitionSpec as P

BLOCK_TOKENS = 512
PIECE = 128
SEED = 16
BATCH = 2
ROWS = 256
TILE = 512
GROUPS = 2
FAR = -1e30
VMEM_BYTES = 36 * 2**20
PREPARE_BYTES = 60 * 2**20
COST = 1.15e9


def lasting(microseconds):
    return pl.CostEstimate(flops=int(microseconds * COST), bytes_accessed=1000, transcendentals=0)


def split(value):
    high = value.astype(jnp.bfloat16)
    return high, (value - high.astype(jnp.float32)).astype(jnp.bfloat16)


def product(left, right, left_dim, right_dim):
    left_high, left_low = split(left)
    right_high, right_low = split(right)
    return lax.dot_general(
        jnp.concatenate([left_high, left_low, left_high], axis=left_dim),
        jnp.concatenate([right_high, right_high, right_low], axis=right_dim),
        (((left_dim,), (right_dim,)), ((), ())),
        preferred_element_type=jnp.float32,
    )


def mm(left, right):
    return product(left, right, 1, 0)


def mm_nt(left, right):
    return product(left, right, 1, 1)


def mm_tn(left, right):
    return product(left, right, 0, 0)


def columns_of(row):
    parts = [
        jnp.broadcast_to(row[:, i : i + PIECE], (PIECE, PIECE)).T
        for i in range(0, row.shape[1], PIECE)
    ]
    return jnp.concatenate(parts, axis=0) if len(parts) > 1 else parts[0]


def unit_lower_inverses(stricts):
    order = stricts[0].shape[0]
    blocks = order // SEED
    rows = lax.broadcasted_iota(jnp.int32, (order, order), 0)
    cols = lax.broadcasted_iota(jnp.int32, (order, order), 1)
    diagonal = rows // SEED == cols // SEED
    packed = []
    for strict in stricts:
        kept = jnp.where(diagonal, strict, 0.0)
        total = kept[:SEED]
        for block in range(1, blocks):
            total = total + kept[block * SEED : (block + 1) * SEED]
        packed.append(total)
    packed = jnp.concatenate(packed, axis=0)
    lane = lax.broadcasted_iota(jnp.int32, packed.shape, 1)
    row = lax.broadcasted_iota(jnp.int32, packed.shape, 0)
    shape = (len(stricts), SEED, order)
    inverse = jnp.where(lane % SEED == row % SEED, 1.0, 0.0).reshape(shape)
    first = lane - lane % SEED
    for k in range(SEED - 1):
        column = jnp.take_along_axis(packed, first + k, axis=1, mode="promise_in_bounds")
        inverse = inverse - column.reshape(shape) * inverse[:, k : k + 1, :]
    inverses = [
        jnp.where(diagonal, jnp.concatenate([inverse[i]] * blocks, axis=0), 0.0)
        for i in range(len(stricts))
    ]
    size = SEED
    while size < order:
        below = (rows // size == cols // size + 1) & (rows // (2 * size) == cols // (2 * size))
        right = [mm(jnp.where(below, s, 0.0), x) for s, x in zip(stricts, inverses)]
        inverses = [x - mm(x, r) for x, r in zip(inverses, right)]
        size *= 2
    return inverses


def stacked_values(values):
    return jnp.concatenate(split(values), axis=1)


def softmax_part(scores, stacked):
    rows, dh = scores.shape[0], stacked.shape[1] // 2
    peak = jnp.max(scores, axis=-1, keepdims=True)
    weights = jnp.exp2(scores - peak)
    total = jnp.sum(weights, axis=-1, keepdims=True)
    summed = lax.dot_general(
        jnp.concatenate(split(weights), axis=0), stacked, (((1,), (0,)), ((), ())),
        preferred_element_type=jnp.float32,
    )
    summed = summed[:rows] + summed[rows:]
    return (summed[:, :dh] + summed[:, dh:]) / total, peak + jnp.log2(total)


def stacked_keys(keys):
    high, low = split(keys)
    return jnp.concatenate([high, high, low], axis=1).T


def stacked_queries(queries):
    high, low = split(queries)
    return jnp.concatenate([high, low, high], axis=1)


def scored(queries, keys):
    return lax.dot_general(queries, keys, (((1,), (0,)), ((), ())), preferred_element_type=jnp.float32)


def prepare_kernel(q_ref, k_ref, v_ref, w_ref, beta_ref, doc_ref, qo_ref, ko_ref, st_ref, o_ref, lse_ref, *, scale):
    batch, dh, _ = st_ref.shape
    length = q_ref.shape[0]
    pieces = length // PIECE
    rows = lax.broadcasted_iota(jnp.int32, (PIECE, PIECE), 0)
    cols = lax.broadcasted_iota(jnp.int32, (PIECE, PIECE), 1)
    identity = jnp.where(rows == cols, 1.0, 0.0)
    spans = [slice(i * PIECE, (i + 1) * PIECE) for i in range(pieces)]
    heads = [slice(h * dh, (h + 1) * dh) for h in range(batch)]
    where = [(head, span) for head in heads for span in spans]
    directions = [w_ref[span, head] for head, span in where]
    units = [w * lax.rsqrt(jnp.sum(w * w, axis=-1, keepdims=True) + 1e-06) for w in directions]
    first = pl.program_id(0) * batch
    beta_rows = [beta_ref[pl.ds(first + h, 1), :] for h in range(batch)]
    betas = [columns_of(row[:, span]) for row in beta_rows for span in spans]
    grams = [
        mm_nt(jnp.concatenate([t, q_ref[span, head]], axis=0), jnp.concatenate([t, k_ref[span, head]], axis=0))
        for t, (head, span) in zip(units, where)
    ]
    inverses = unit_lower_inverses(
        [jnp.where(rows > cols, beta * g[:PIECE, :PIECE], 0.0) for beta, g in zip(betas, grams)]
    )
    solved = [
        mm(x, jnp.concatenate([jnp.where(rows > cols, beta * g[:PIECE, PIECE:], 0.0), beta * t], axis=1))
        for x, beta, g, t in zip(inverses, betas, grams, units)
    ]
    change = [mm(jnp.where(rows >= cols, g[PIECE:, :PIECE], 0.0), s) for g, s in zip(grams, solved)]
    carried = [mm_tn(s, t) for s, t in zip(solved, units)]

    def by_head(flat):
        return [flat[h * pieces : (h + 1) * pieces] for h in range(batch)]

    own = by_head([g[PIECE:, PIECE:] - c[:, :PIECE] for g, c in zip(grams, change)])
    q_hat = by_head([q_ref[span, head] - c[:, PIECE:] for (head, span), c in zip(where, change)])
    k_hat = by_head([k_ref[span, head] - c[:PIECE] for (head, span), c in zip(where, carried)])
    st = by_head([identity - c[PIECE:] for c in carried])
    tiles = [[[None] * pieces for _ in range(pieces)] for _ in range(batch)]
    for h in range(batch):
        for i in range(pieces):
            tiles[h][i][i] = own[h][i]
    current = [list(q) for q in q_hat]
    suffix = [[None] * pieces for _ in range(batch)]
    for back in range(1, pieces):
        for h in range(batch):
            for i in range(back, pieces):
                tiles[h][i][i - back] = mm_nt(current[h][i], k_hat[h][i - back])
                current[h][i] = mm_nt(current[h][i], st[h][i - back])
            j = pieces - back
            suffix[h][j - 1] = st[h][j] if back == 1 else mm(st[h][j], suffix[h][j])
    for h in range(batch):
        for i in range(pieces):
            qo_ref[h, spans[i], :] = current[h][i]
            ko_ref[h, spans[i], :] = k_hat[h][i] if i == pieces - 1 else mm(k_hat[h][i], suffix[h][i])
        st_ref[h] = mm(st[h][0], suffix[h][0]) if pieces > 1 else st[h][0]
    doc_row = (doc_ref[...].reshape(1, length) + 1).astype(jnp.float32)
    doc_col = columns_of(doc_row)
    doc_lines = [doc_row[:, span] for span in spans]
    doc_lines.append(jnp.zeros((qo_ref.shape[1] - length - pieces, dh), jnp.float32))
    doc_lines = jnp.concatenate(doc_lines, axis=0)
    for h in range(batch):
        qo_ref[h, length:, :] = doc_lines
        ko_ref[h, length:, :] = doc_lines
    stacked = [stacked_values(v_ref[:, head]) for head in heads]
    for i in range(pieces):
        for h in range(batch):
            masked = []
            for j in range(i + 1):
                same = doc_col[spans[i]] == doc_row[:, spans[j]]
                if i == j:
                    same = same & (rows >= cols)
                masked.append(jnp.where(same, tiles[h][i][j] * scale, FAR))
            out, lse = softmax_part(
                jnp.concatenate(masked, axis=1) if i else masked[0], stacked[h][: (i + 1) * PIECE]
            )
            o_ref[h, spans[i], :] = out
            lse_ref[h, spans[i], :] = jnp.broadcast_to(lse, (PIECE, PIECE))


def message_rows(length):
    return length + (length // PIECE + 7) // 8 * 8


def prepare(queries, keys, values, transitions, betas, documents, scale):
    length = queries.shape[0]
    heads = betas.shape[0]
    dh = queries.shape[1] // heads
    rows = message_rows(length)
    column = pl.BlockSpec((length, BATCH * dh), lambda h: (0, h))
    head = pl.BlockSpec((BATCH, length, dh), lambda h: (h, 0, 0))
    message = pl.BlockSpec((BATCH, rows, dh), lambda h: (h, 0, 0))
    f32 = jnp.float32
    return pl.pallas_call(
        functools.partial(prepare_kernel, scale=scale),
        grid=(heads // BATCH,),
        in_specs=[column] * 4
        + [
            pl.BlockSpec((heads, length), lambda h: (0, 0)),
            pl.BlockSpec((length,), lambda h: (0,)),
        ],
        out_specs=[message, message, pl.BlockSpec((BATCH, dh, dh), lambda h: (h, 0, 0)), head, head],
        out_shape=[
            jax.ShapeDtypeStruct((heads, rows, dh), f32),
            jax.ShapeDtypeStruct((heads, rows, dh), f32),
            jax.ShapeDtypeStruct((heads, dh, dh), f32),
            jax.ShapeDtypeStruct((heads, length, dh), f32),
            jax.ShapeDtypeStruct((heads, length, dh), f32),
        ],
        compiler_params=pltpu.CompilerParams(vmem_limit_bytes=PREPARE_BYTES),
        name="prepare",
        cost_estimate=lasting(13),
    )(queries, keys, values, transitions, betas, documents)


def steps_kernel(place_ref, own_ref, near_ref, out_ref):
    even = lax.rem(place_ref[0], 2) == 0
    for h in range(own_ref.shape[0]):
        near = near_ref[h]
        out_ref[h] = jnp.where(even, near, mm(near, own_ref[h]))


def joined_steps(place, own, near):
    whole = pl.BlockSpec(own.shape, lambda i, p: (0, 0, 0))
    return pl.pallas_call(
        steps_kernel,
        grid_spec=pltpu.PrefetchScalarGridSpec(
            num_scalar_prefetch=1, grid=(1,), in_specs=[whole, whole], out_specs=whole
        ),
        out_shape=jax.ShapeDtypeStruct(own.shape, jnp.float32),
        compiler_params=pltpu.CompilerParams(vmem_limit_bytes=VMEM_BYTES),
        name="joined_steps",
        cost_estimate=lasting(2),
    )(place, own, near)


def doc_line(ref, length, valid):
    line = jnp.concatenate([ref[0, length + i : length + i + 1, :] for i in range(length // PIECE)], axis=1)
    return jnp.where(valid, line, 0.0)


def masked(scores, col, row):
    wide = jnp.concatenate([col] * (scores.shape[1] // PIECE), axis=1)
    return jnp.where(wide == row, scores, FAR)


def attended_part(query, keys, values, docs, col):
    parts = []
    for start in range(0, query.shape[0], ROWS):
        span = slice(start, start + ROWS)
        parts.append((span, *softmax_part(masked(scored(query[span], keys), col[span], docs), values)))
    return parts


def joined_parts(out, lse, other, other_lse):
    peak = jnp.maximum(lse, other_lse)
    w, w_other = jnp.exp2(lse - peak), jnp.exp2(other_lse - peak)
    total = w + w_other
    return (out * w + other * w_other) / total, peak + jnp.log2(total)


def early_kernel(place_ref, qp_ref, ko_ref, vo_ref, k2_ref, v2a_ref, v2b_ref, u_ref, out_ref, lse_ref, *, scale):
    length, dh = vo_ref.shape
    place = place_ref[0]
    pick = lambda a, b: jnp.where(lax.rem(place, 2) == 0, a, b)
    docs = pick(doc_line(ko_ref, length, True), doc_line(k2_ref, length, place >= 4))
    keys = stacked_keys(pick(ko_ref[0, :length, :], mm(k2_ref[0, :length, :], u_ref[0])))
    values = stacked_values(
        pick(vo_ref[...], jnp.concatenate([v2a_ref[...], v2b_ref[...]], axis=0))
    )
    query = stacked_queries(qp_ref[0, :length, :] * scale)
    col = columns_of(doc_line(qp_ref, length, True))
    for span, out, lse in attended_part(query, keys, values, docs, col):
        out_ref[0, span, :] = out
        lse_ref[0, span, :] = jnp.broadcast_to(lse, (ROWS, dh))


def late_kernel(place_ref, qp_ref, k1_ref, v1a_ref, v1b_ref, s_ref, u_ref, oe_ref, le_ref, msg_ref, *, scale):
    length = oe_ref.shape[1]
    place = place_ref[0]
    pick = lambda a, b: jnp.where(lax.rem(place, 2) == 0, a, b)
    docs = doc_line(k1_ref, length, place >= 2)
    k1 = k1_ref[0, :length, :]
    keys = stacked_keys(pick(mm(k1, u_ref[0]), k1))
    values = stacked_values(jnp.concatenate([v1a_ref[...], v1b_ref[...]], axis=0))
    query = qp_ref[0, :length, :] * scale
    query = stacked_queries(pick(mm_nt(query, s_ref[0]), query))
    col = columns_of(doc_line(qp_ref, length, True))
    for span, out, lse in attended_part(query, keys, values, docs, col):
        out, lse = joined_parts(out, lse, oe_ref[0, span, :], le_ref[0, span, :])
        msg_ref[0, span, :] = out
        for i in range(0, ROWS, PIECE):
            line = length + (span.start + i) // PIECE
            msg_ref[0, line : line + 1, :] = lse[i : i + PIECE].T[:1]
    first = length + length // PIECE
    msg_ref[0, first:, :] = jnp.zeros((msg_ref.shape[1] - first, msg_ref.shape[2]), jnp.float32)


def own_kernel(place_ref, qo_ref, k1_ref, v1a_ref, v1b_ref, s_ref, u_ref, od_ref, ld_ref, out_ref, lse_ref, *, scale):
    length = od_ref.shape[1]
    place = place_ref[0]
    even = lax.rem(place, 2) == 0
    pick = lambda a, b: jnp.where(even, a, b)
    docs = doc_line(k1_ref, length, place >= 2)
    k1 = k1_ref[0, :length, :]
    keys = stacked_keys(pick(mm(k1, u_ref[0]), k1))
    values = stacked_values(jnp.concatenate([v1a_ref[...], v1b_ref[...]], axis=0))
    query = qo_ref[0, :length, :] * scale
    query = stacked_queries(pick(query, mm_nt(query, s_ref[0])))
    col = columns_of(doc_line(qo_ref, length, True))
    for span, out, lse in attended_part(query, keys, values, docs, col):
        out, lse = joined_parts(out, lse, od_ref[0, span, :], ld_ref[0, span, :])
        out_ref[0, span, :] = out
        lse_ref[0, span, :] = lse


def cross_specs(group, per_group, length, rows, dh):
    return {
        "all": pl.BlockSpec((1, rows, dh), lambda h, p: (group * per_group + h, 0, 0)),
        "part": pl.BlockSpec((1, rows, dh), lambda h, p: (h, 0, 0)),
        "all_values": pl.BlockSpec((length, dh), lambda h, p: (0, group * per_group + h)),
        "half_values": pl.BlockSpec((length // 2, dh), lambda h, p: (0, group * per_group + h)),
        "step": pl.BlockSpec((1, dh, dh), lambda h, p: (group * per_group + h, 0, 0)),
        "all_plain": pl.BlockSpec((1, length, dh), lambda h, p: (group * per_group + h, 0, 0)),
        "plain": pl.BlockSpec((1, length, dh), lambda h, p: (h, 0, 0)),
    }


def early_part(group, per_group, place, q_near, k_own, values, k2, v2, joined, scale):
    length = values.shape[0]
    _, rows, dh = q_near.shape
    spec = cross_specs(group, per_group, length, rows, dh)
    names = ["all", "all", "all_values", "part", "half_values", "half_values", "step"]
    shape = jax.ShapeDtypeStruct((per_group, length, dh), jnp.float32)
    return pl.pallas_call(
        functools.partial(early_kernel, scale=scale),
        grid_spec=pltpu.PrefetchScalarGridSpec(
            num_scalar_prefetch=1,
            grid=(per_group,),
            in_specs=[spec[name] for name in names],
            out_specs=[spec["plain"], spec["plain"]],
        ),
        out_shape=[shape, shape],
        compiler_params=pltpu.CompilerParams(vmem_limit_bytes=VMEM_BYTES),
        name="early",
        cost_estimate=lasting(4.5),
    )(place, q_near, k_own, values, k2, *v2, joined)


def late_part(group, per_group, place, q_near, k1, v1, steps, joined, early, scale):
    _, rows, dh = q_near.shape
    length = early[0].shape[1]
    spec = cross_specs(group, per_group, length, rows, dh)
    names = ["all", "part", "half_values", "half_values", "step", "step", "plain", "plain"]
    return pl.pallas_call(
        functools.partial(late_kernel, scale=scale),
        grid_spec=pltpu.PrefetchScalarGridSpec(
            num_scalar_prefetch=1,
            grid=(per_group,),
            in_specs=[spec[name] for name in names],
            out_specs=spec["part"],
        ),
        out_shape=jax.ShapeDtypeStruct((per_group, rows, dh), jnp.float32),
        compiler_params=pltpu.CompilerParams(vmem_limit_bytes=VMEM_BYTES),
        name="late",
        cost_estimate=lasting(4.5),
    )(place, q_near, k1, *v1, steps, joined, *early)


def own_part(group, per_group, place, q_own, k1, v1, near_steps, joined, od, ld, scale):
    length = od.shape[1]
    _, rows, dh = q_own.shape
    spec = cross_specs(group, per_group, length, rows, dh)
    names = ["all", "part", "half_values", "half_values", "step", "step", "all_plain", "all_plain"]
    shape = jax.ShapeDtypeStruct((per_group, length, dh), jnp.float32)
    return pl.pallas_call(
        functools.partial(own_kernel, scale=scale),
        grid_spec=pltpu.PrefetchScalarGridSpec(
            num_scalar_prefetch=1,
            grid=(per_group,),
            in_specs=[spec[name] for name in names],
            out_specs=[spec["plain"], spec["plain"]],
        ),
        out_shape=[shape, shape],
        compiler_params=pltpu.CompilerParams(vmem_limit_bytes=VMEM_BYTES),
        name="own",
        cost_estimate=lasting(4.5),
    )(place, q_own, k1, *v1, near_steps, joined, od, ld)


def merge_kernel(core_ref, o_ref, lse_ref, msg_ref, keep_ref, send_ref):
    length, dh = o_ref.shape[1:]
    share = keep_ref.shape[0]
    parts = []
    for i in range(length // PIECE):
        span = slice(i * PIECE, (i + 1) * PIECE)
        lse = lse_ref[0, span, :]
        lse_p = columns_of(msg_ref[0, length + i : length + i + 1, :])
        peak = jnp.maximum(lse, lse_p)
        w, w_p = jnp.exp2(lse - peak), jnp.exp2(lse_p - peak)
        parts.append((o_ref[0, span, :] * w + msg_ref[0, span, :] * w_p) / (w + w_p))
    whole = jnp.concatenate(parts, axis=0)
    first = core_ref[0] == 0
    low, high = whole[:share], whole[share:]
    keep_ref[...] = jnp.where(first, low, high)
    send_ref[...] = jnp.where(first, high, low)


def merge(core, o, lse, msg):
    per_group, length, dh = o.shape
    share = length // 2
    head = pl.BlockSpec((1, length, dh), lambda h, c: (h, 0, 0))
    out = pl.BlockSpec((share, dh), lambda h, c: (0, h))
    shape = jax.ShapeDtypeStruct((share, per_group * dh), jnp.float32)
    return pl.pallas_call(
        merge_kernel,
        grid_spec=pltpu.PrefetchScalarGridSpec(
            num_scalar_prefetch=1,
            grid=(per_group,),
            in_specs=[head, head, pl.BlockSpec((1,) + msg.shape[1:], lambda h, c: (h, 0, 0))],
            out_specs=[out, out],
        ),
        out_shape=[shape, shape],
        compiler_params=pltpu.CompilerParams(vmem_limit_bytes=VMEM_BYTES),
        name="merge",
        cost_estimate=lasting(2.2),
    )(core, o, lse, msg)


def halves_kernel(own_ref, other_ref, *out_refs):
    for ref, (high, low) in zip((own_ref, other_ref), (out_refs[:2], out_refs[2:])):
        high[pl.program_id(0)], low[pl.program_id(0)] = split(ref[...])


def weight_halves(w_own, w_other):
    depth, width = w_own.shape
    tile = min(width, TILE)
    spec = pl.BlockSpec((depth, tile), lambda n: (0, n))
    kept = pl.BlockSpec(memory_space=pltpu.VMEM)
    return pl.pallas_call(
        halves_kernel,
        grid=(width // tile,),
        in_specs=[spec] * 2,
        out_specs=[kept] * 4,
        out_shape=[pltpu.VMEM((width // tile, depth, tile), jnp.bfloat16)] * 4,
        compiler_params=pltpu.CompilerParams(vmem_limit_bytes=VMEM_BYTES),
        name="weight_halves",
        cost_estimate=lasting(7),
    )(w_own, w_other)


def project_kernel(*refs):
    *a_refs, own_high, own_low, other_high, other_low, out_ref = refs
    half = len(a_refs) // 2
    parts = []
    for part, high, low in ((a_refs[:half], own_high, own_low), (a_refs[half:], other_high, other_low)):
        a_high, a_low = split(jnp.concatenate([r[...] for r in part], axis=1))
        stacked = scored(jnp.concatenate([a_high, a_low], axis=0), high[pl.program_id(0)])
        rows = a_high.shape[0]
        parts.append(stacked[:rows] + (stacked[rows:] + scored(a_high, low[pl.program_id(0)])))
    out_ref[...] = parts[0] + parts[1]


def project(kept, received, weights):
    share = kept[0].shape[0]
    tiles, depth, tile = weights[0].shape
    width = tiles * tile
    a_spec = [pl.BlockSpec(a.shape, lambda n: (0, 0)) for a in kept + received]
    w_spec = pl.BlockSpec(memory_space=pltpu.VMEM)
    return pl.pallas_call(
        project_kernel,
        grid=(tiles,),
        in_specs=a_spec + [w_spec] * 4,
        out_specs=pl.BlockSpec((share, tile), lambda n: (0, n)),
        out_shape=jax.ShapeDtypeStruct((share, width), jnp.float32),
        compiler_params=pltpu.CompilerParams(vmem_limit_bytes=VMEM_BYTES),
        name="project",
        cost_estimate=lasting(7.5),
    )(*kept, *received, *weights)


def onward(value, steps):
    count = lax.axis_size("ctx")
    return lax.ppermute(value, "ctx", [(i, (i + steps) % count) for i in range(count)])


def exchanged(value, axis, bit):
    return lax.ppermute(value, axis, [(i, i ^ bit) for i in range(lax.axis_size(axis))])


def after(value, *others):
    return lax.optimization_barrier((value,) + others)[0]


def shards(queries, keys, values, transitions, betas, documents, out_weight):
    heads, length = betas.shape
    dh = queries.shape[1] // heads
    assert length == BLOCK_TOKENS and lax.axis_size("ctx") % 4 == 0 and lax.axis_size("head") == 2
    per_group = heads // GROUPS
    groups = range(GROUPS)
    scale = math.log2(math.e) / math.sqrt(dh)
    index = lax.axis_index("ctx").astype(jnp.int32)
    place = index.reshape(1)
    core = lax.axis_index("head").astype(jnp.int32).reshape(1)
    far_side = lax.rem(index, 4) >= 2
    v_first, v_last = values[: length // 2], values[length // 2 :]

    def chosen(block, behind):
        return jnp.where(far_side, behind, block)

    v2_first = onward(v_first, 4)
    w_other = exchanged(out_weight, "head", 1)
    prepared = prepare(queries, keys, values, transitions, betas, documents, scale)
    q_msg, k_msg, steps, od, ld, v2_first, w_other = lax.optimization_barrier((*prepared, v2_first, w_other))
    own_k = [k_msg[g * per_group : (g + 1) * per_group] for g in groups]
    near_steps = exchanged(steps, "ctx", 1)
    v1_first = exchanged(chosen(v_first, v2_first), "ctx", 2)
    v2_last = onward(after(v_last, steps), 4)
    q_near = exchanged(after(q_msg, near_steps), "ctx", 1)
    joined = joined_steps(place, steps, near_steps)
    joined = onward(joined, 2)
    source = chosen(v_last, v2_last)
    v1_last = exchanged(source, "ctx", 2)
    k2 = [onward(after(own_k[0], source), 4)]
    k2 += [onward(after(block, joined, source), 4) for block in own_k[1:]]
    weights = weight_halves(out_weight, after(w_other, joined, source))
    sources = [chosen(after(own_k[0], v1_first, v1_last), k2[0])]
    v1, v2 = (v1_first, v1_last), (v2_first, v2_last)
    early = []
    for g in groups:
        if g:
            sources.append(chosen(after(own_k[g], early[-1][0]), k2[g]))
        ready = after(place, sources[g], *weights)
        early.append(early_part(g, per_group, ready, q_near, k_msg, values, k2[g], v2, joined, scale))
    k1 = [exchanged(source, "ctx", 2) for source in sources]
    kept, received = [], []
    for g in groups:
        msg = late_part(g, per_group, place, q_near, k1[g], v1, steps, joined, early[g], scale)
        out, lse = own_part(g, per_group, place, q_msg, k1[g], v1, near_steps, joined, od, ld, scale)
        keep, send = merge(core, out, lse, exchanged(msg, "ctx", 1))
        kept.append(keep)
        received.append(exchanged(send, "head", 1))
    return project(kept, received, weights)


def solution(mesh):
    return jax.shard_map(
        shards,
        mesh=mesh,
        in_specs=(
            P("ctx", "head"),
            P("ctx", "head"),
            P("ctx", "head"),
            P("ctx", "head"),
            P("head", "ctx"),
            P("ctx"),
            P("head", None),
        ),
        out_specs=P(("ctx", "head"), None),
        check_vma=False,
    )
```

```python
import functools
import math

import jax
import jax.numpy as jnp
from jax import lax
from jax.experimental import pallas as pl
from jax.experimental.pallas import tpu as pltpu
from jax.sharding import PartitionSpec as P

BLOCK_TOKENS = 512
PIECE = 128
SEED = 16
BATCH = 2
ROWS = 256
TILE = 512
GROUPS = 2
FAR = -1e30
VMEM_BYTES = 36 * 2**20
PREPARE_BYTES = 60 * 2**20
COST = 1.15e9


def lasting(microseconds):
    return pl.CostEstimate(flops=int(microseconds * COST), bytes_accessed=1000, transcendentals=0)


def split(value):
    high = value.astype(jnp.bfloat16)
    return high, (value - high.astype(jnp.float32)).astype(jnp.bfloat16)


def product(left, right, left_dim, right_dim):
    left_high, left_low = split(left)
    right_high, right_low = split(right)
    return lax.dot_general(
        jnp.concatenate([left_high, left_low, left_high], axis=left_dim),
        jnp.concatenate([right_high, right_high, right_low], axis=right_dim),
        (((left_dim,), (right_dim,)), ((), ())),
        preferred_element_type=jnp.float32,
    )


def mm(left, right):
    return product(left, right, 1, 0)


def mm_nt(left, right):
    return product(left, right, 1, 1)


def mm_tn(left, right):
    return product(left, right, 0, 0)


def columns_of(row):
    parts = [
        jnp.broadcast_to(row[:, i : i + PIECE], (PIECE, PIECE)).T
        for i in range(0, row.shape[1], PIECE)
    ]
    return jnp.concatenate(parts, axis=0) if len(parts) > 1 else parts[0]


def unit_lower_inverses(stricts):
    order = stricts[0].shape[0]
    blocks = order // SEED
    rows = lax.broadcasted_iota(jnp.int32, (order, order), 0)
    cols = lax.broadcasted_iota(jnp.int32, (order, order), 1)
    diagonal = rows // SEED == cols // SEED
    packed = []
    for strict in stricts:
        kept = jnp.where(diagonal, strict, 0.0)
        total = kept[:SEED]
        for block in range(1, blocks):
            total = total + kept[block * SEED : (block + 1) * SEED]
        packed.append(total)
    packed = jnp.concatenate(packed, axis=0)
    lane = lax.broadcasted_iota(jnp.int32, packed.shape, 1)
    row = lax.broadcasted_iota(jnp.int32, packed.shape, 0)
    shape = (len(stricts), SEED, order)
    inverse = jnp.where(lane % SEED == row % SEED, 1.0, 0.0).reshape(shape)
    first = lane - lane % SEED
    for k in range(SEED - 1):
        column = jnp.take_along_axis(packed, first + k, axis=1, mode="promise_in_bounds")
        inverse = inverse - column.reshape(shape) * inverse[:, k : k + 1, :]
    inverses = [
        jnp.where(diagonal, jnp.concatenate([inverse[i]] * blocks, axis=0), 0.0)
        for i in range(len(stricts))
    ]
    size = SEED
    while size < order:
        below = (rows // size == cols // size + 1) & (rows // (2 * size) == cols // (2 * size))
        right = [mm(jnp.where(below, s, 0.0), x) for s, x in zip(stricts, inverses)]
        inverses = [x - mm(x, r) for x, r in zip(inverses, right)]
        size *= 2
    return inverses


def stacked_values(values):
    return jnp.concatenate(split(values), axis=1)


def softmax_part(scores, stacked):
    rows, dh = scores.shape[0], stacked.shape[1] // 2
    peak = jnp.max(scores, axis=-1, keepdims=True)
    weights = jnp.exp2(scores - peak)
    total = jnp.sum(weights, axis=-1, keepdims=True)
    summed = lax.dot_general(
        jnp.concatenate(split(weights), axis=0), stacked, (((1,), (0,)), ((), ())),
        preferred_element_type=jnp.float32,
    )
    summed = summed[:rows] + summed[rows:]
    return (summed[:, :dh] + summed[:, dh:]) / total, peak + jnp.log2(total)


def stacked_keys(keys):
    high, low = split(keys)
    return jnp.concatenate([high, high, low], axis=1).T


def stacked_queries(queries):
    high, low = split(queries)
    return jnp.concatenate([high, low, high], axis=1)


def scored(queries, keys):
    return lax.dot_general(queries, keys, (((1,), (0,)), ((), ())), preferred_element_type=jnp.float32)


def prepare_kernel(q_ref, k_ref, v_ref, w_ref, beta_ref, doc_ref, qo_ref, ko_ref, st_ref, o_ref, lse_ref, *, scale):
    batch, dh, _ = st_ref.shape
    length = q_ref.shape[0]
    pieces = length // PIECE
    rows = lax.broadcasted_iota(jnp.int32, (PIECE, PIECE), 0)
    cols = lax.broadcasted_iota(jnp.int32, (PIECE, PIECE), 1)
    identity = jnp.where(rows == cols, 1.0, 0.0)
    spans = [slice(i * PIECE, (i + 1) * PIECE) for i in range(pieces)]
    heads = [slice(h * dh, (h + 1) * dh) for h in range(batch)]
    where = [(head, span) for head in heads for span in spans]
    directions = [w_ref[span, head] for head, span in where]
    units = [w * lax.rsqrt(jnp.sum(w * w, axis=-1, keepdims=True) + 1e-06) for w in directions]
    first = pl.program_id(0) * batch
    beta_rows = [beta_ref[pl.ds(first + h, 1), :] for h in range(batch)]
    betas = [columns_of(row[:, span]) for row in beta_rows for span in spans]
    grams = [
        mm_nt(jnp.concatenate([t, q_ref[span, head]], axis=0), jnp.concatenate([t, k_ref[span, head]], axis=0))
        for t, (head, span) in zip(units, where)
    ]
    inverses = unit_lower_inverses(
        [jnp.where(rows > cols, beta * g[:PIECE, :PIECE], 0.0) for beta, g in zip(betas, grams)]
    )
    solved = [
        mm(x, jnp.concatenate([jnp.where(rows > cols, beta * g[:PIECE, PIECE:], 0.0), beta * t], axis=1))
        for x, beta, g, t in zip(inverses, betas, grams, units)
    ]
    change = [mm(jnp.where(rows >= cols, g[PIECE:, :PIECE], 0.0), s) for g, s in zip(grams, solved)]
    carried = [mm_tn(s, t) for s, t in zip(solved, units)]

    def by_head(flat):
        return [flat[h * pieces : (h + 1) * pieces] for h in range(batch)]

    own = by_head([g[PIECE:, PIECE:] - c[:, :PIECE] for g, c in zip(grams, change)])
    q_hat = by_head([q_ref[span, head] - c[:, PIECE:] for (head, span), c in zip(where, change)])
    k_hat = by_head([k_ref[span, head] - c[:PIECE] for (head, span), c in zip(where, carried)])
    st = by_head([identity - c[PIECE:] for c in carried])
    tiles = [[[None] * pieces for _ in range(pieces)] for _ in range(batch)]
    for h in range(batch):
        for i in range(pieces):
            tiles[h][i][i] = own[h][i]
    current = [list(q) for q in q_hat]
    suffix = [[None] * pieces for _ in range(batch)]
    for back in range(1, pieces):
        for h in range(batch):
            for i in range(back, pieces):
                tiles[h][i][i - back] = mm_nt(current[h][i], k_hat[h][i - back])
                current[h][i] = mm_nt(current[h][i], st[h][i - back])
            j = pieces - back
            suffix[h][j - 1] = st[h][j] if back == 1 else mm(st[h][j], suffix[h][j])
    for h in range(batch):
        for i in range(pieces):
            qo_ref[h, spans[i], :] = current[h][i]
            ko_ref[h, spans[i], :] = k_hat[h][i] if i == pieces - 1 else mm(k_hat[h][i], suffix[h][i])
        st_ref[h] = mm(st[h][0], suffix[h][0]) if pieces > 1 else st[h][0]
    doc_row = (doc_ref[...].reshape(1, length) + 1).astype(jnp.float32)
    doc_col = columns_of(doc_row)
    doc_lines = [doc_row[:, span] for span in spans]
    doc_lines.append(jnp.zeros((qo_ref.shape[1] - length - pieces, dh), jnp.float32))
    doc_lines = jnp.concatenate(doc_lines, axis=0)
    for h in range(batch):
        qo_ref[h, length:, :] = doc_lines
        ko_ref[h, length:, :] = doc_lines
    stacked = [stacked_values(v_ref[:, head]) for head in heads]
    for i in range(pieces):
        for h in range(batch):
            masked = []
            for j in range(i + 1):
                same = doc_col[spans[i]] == doc_row[:, spans[j]]
                if i == j:
                    same = same & (rows >= cols)
                masked.append(jnp.where(same, tiles[h][i][j] * scale, FAR))
            out, lse = softmax_part(
                jnp.concatenate(masked, axis=1) if i else masked[0], stacked[h][: (i + 1) * PIECE]
            )
            o_ref[h, spans[i], :] = out
            lse_ref[h, spans[i], :] = jnp.broadcast_to(lse, (PIECE, PIECE))


def message_rows(length):
    return length + (length // PIECE + 7) // 8 * 8


def prepare(queries, keys, values, transitions, betas, documents, scale):
    length = queries.shape[0]
    heads = betas.shape[0]
    dh = queries.shape[1] // heads
    rows = message_rows(length)
    column = pl.BlockSpec((length, BATCH * dh), lambda h: (0, h))
    head = pl.BlockSpec((BATCH, length, dh), lambda h: (h, 0, 0))
    message = pl.BlockSpec((BATCH, rows, dh), lambda h: (h, 0, 0))
    f32 = jnp.float32
    return pl.pallas_call(
        functools.partial(prepare_kernel, scale=scale),
        grid=(heads // BATCH,),
        in_specs=[column] * 4
        + [
            pl.BlockSpec((heads, length), lambda h: (0, 0)),
            pl.BlockSpec((length,), lambda h: (0,)),
        ],
        out_specs=[message, message, pl.BlockSpec((BATCH, dh, dh), lambda h: (h, 0, 0)), head, head],
        out_shape=[
            jax.ShapeDtypeStruct((heads, rows, dh), f32),
            jax.ShapeDtypeStruct((heads, rows, dh), f32),
            jax.ShapeDtypeStruct((heads, dh, dh), f32),
            jax.ShapeDtypeStruct((heads, length, dh), f32),
            jax.ShapeDtypeStruct((heads, length, dh), f32),
        ],
        compiler_params=pltpu.CompilerParams(vmem_limit_bytes=PREPARE_BYTES),
        name="prepare",
        cost_estimate=lasting(13),
    )(queries, keys, values, transitions, betas, documents)


def steps_kernel(place_ref, own_ref, near_ref, out_ref):
    even = lax.rem(place_ref[0], 2) == 0
    for h in range(own_ref.shape[0]):
        near = near_ref[h]
        out_ref[h] = jnp.where(even, near, mm(near, own_ref[h]))


def joined_steps(place, own, near):
    whole = pl.BlockSpec(own.shape, lambda i, p: (0, 0, 0))
    return pl.pallas_call(
        steps_kernel,
        grid_spec=pltpu.PrefetchScalarGridSpec(
            num_scalar_prefetch=1, grid=(1,), in_specs=[whole, whole], out_specs=whole
        ),
        out_shape=jax.ShapeDtypeStruct(own.shape, jnp.float32),
        compiler_params=pltpu.CompilerParams(vmem_limit_bytes=VMEM_BYTES),
        name="joined_steps",
        cost_estimate=lasting(2),
    )(place, own, near)


def doc_line(ref, length, valid):
    line = jnp.concatenate([ref[0, length + i : length + i + 1, :] for i in range(length // PIECE)], axis=1)
    return jnp.where(valid, line, 0.0)


def masked(scores, col, row):
    wide = jnp.concatenate([col] * (scores.shape[1] // PIECE), axis=1)
    return jnp.where(wide == row, scores, FAR)


def attended_part(query, keys, values, docs, col):
    parts = []
    for start in range(0, query.shape[0], ROWS):
        span = slice(start, start + ROWS)
        parts.append((span, *softmax_part(masked(scored(query[span], keys), col[span], docs), values)))
    return parts


def joined_parts(out, lse, other, other_lse):
    peak = jnp.maximum(lse, other_lse)
    w, w_other = jnp.exp2(lse - peak), jnp.exp2(other_lse - peak)
    total = w + w_other
    return (out * w + other * w_other) / total, peak + jnp.log2(total)


def early_kernel(place_ref, qp_ref, ko_ref, vo_ref, k2_ref, v2a_ref, v2b_ref, u_ref, out_ref, lse_ref, *, scale):
    length, dh = vo_ref.shape
    place = place_ref[0]
    pick = lambda a, b: jnp.where(lax.rem(place, 2) == 0, a, b)
    docs = pick(doc_line(ko_ref, length, True), doc_line(k2_ref, length, place >= 4))
    keys = stacked_keys(pick(ko_ref[0, :length, :], mm(k2_ref[0, :length, :], u_ref[0])))
    values = stacked_values(
        pick(vo_ref[...], jnp.concatenate([v2a_ref[...], v2b_ref[...]], axis=0))
    )
    query = stacked_queries(qp_ref[0, :length, :] * scale)
    col = columns_of(doc_line(qp_ref, length, True))
    for span, out, lse in attended_part(query, keys, values, docs, col):
        out_ref[0, span, :] = out
        lse_ref[0, span, :] = jnp.broadcast_to(lse, (ROWS, dh))


def late_kernel(place_ref, qp_ref, k1_ref, v1a_ref, v1b_ref, s_ref, u_ref, oe_ref, le_ref, msg_ref, *, scale):
    length = oe_ref.shape[1]
    place = place_ref[0]
    pick = lambda a, b: jnp.where(lax.rem(place, 2) == 0, a, b)
    docs = doc_line(k1_ref, length, place >= 2)
    k1 = k1_ref[0, :length, :]
    keys = stacked_keys(pick(mm(k1, u_ref[0]), k1))
    values = stacked_values(jnp.concatenate([v1a_ref[...], v1b_ref[...]], axis=0))
    query = qp_ref[0, :length, :] * scale
    query = stacked_queries(pick(mm_nt(query, s_ref[0]), query))
    col = columns_of(doc_line(qp_ref, length, True))
    for span, out, lse in attended_part(query, keys, values, docs, col):
        out, lse = joined_parts(out, lse, oe_ref[0, span, :], le_ref[0, span, :])
        msg_ref[0, span, :] = out
        for i in range(0, ROWS, PIECE):
            line = length + (span.start + i) // PIECE
            msg_ref[0, line : line + 1, :] = lse[i : i + PIECE].T[:1]
    first = length + length // PIECE
    msg_ref[0, first:, :] = jnp.zeros((msg_ref.shape[1] - first, msg_ref.shape[2]), jnp.float32)


def own_kernel(place_ref, qo_ref, k1_ref, v1a_ref, v1b_ref, s_ref, u_ref, od_ref, ld_ref, out_ref, lse_ref, *, scale):
    length = od_ref.shape[1]
    place = place_ref[0]
    even = lax.rem(place, 2) == 0
    pick = lambda a, b: jnp.where(even, a, b)
    docs = doc_line(k1_ref, length, place >= 2)
    k1 = k1_ref[0, :length, :]
    keys = stacked_keys(pick(mm(k1, u_ref[0]), k1))
    values = stacked_values(jnp.concatenate([v1a_ref[...], v1b_ref[...]], axis=0))
    query = qo_ref[0, :length, :] * scale
    query = stacked_queries(pick(query, mm_nt(query, s_ref[0])))
    col = columns_of(doc_line(qo_ref, length, True))
    for span, out, lse in attended_part(query, keys, values, docs, col):
        out, lse = joined_parts(out, lse, od_ref[0, span, :], ld_ref[0, span, :])
        out_ref[0, span, :] = out
        lse_ref[0, span, :] = lse


def cross_specs(group, per_group, length, rows, dh, skip=0):
    return {
        "all": pl.BlockSpec((1, rows, dh), lambda h, p: (group * per_group + skip + h, 0, 0)),
        "part": pl.BlockSpec((1, rows, dh), lambda h, p: (skip + h, 0, 0)),
        "all_values": pl.BlockSpec((length, dh), lambda h, p: (0, group * per_group + skip + h)),
        "half_values": pl.BlockSpec((length // 2, dh), lambda h, p: (0, group * per_group + skip + h)),
        "step": pl.BlockSpec((1, dh, dh), lambda h, p: (group * per_group + skip + h, 0, 0)),
        "all_plain": pl.BlockSpec((1, length, dh), lambda h, p: (group * per_group + skip + h, 0, 0)),
        "plain": pl.BlockSpec((1, length, dh), lambda h, p: (skip + h, 0, 0)),
    }


def early_part(group, per_group, place, q_near, k_own, values, k2, v2, joined, scale):
    length = values.shape[0]
    _, rows, dh = q_near.shape
    spec = cross_specs(group, per_group, length, rows, dh)
    names = ["all", "all", "all_values", "part", "half_values", "half_values", "step"]
    shape = jax.ShapeDtypeStruct((per_group, length, dh), jnp.float32)
    return pl.pallas_call(
        functools.partial(early_kernel, scale=scale),
        grid_spec=pltpu.PrefetchScalarGridSpec(
            num_scalar_prefetch=1,
            grid=(per_group,),
            in_specs=[spec[name] for name in names],
            out_specs=[spec["plain"], spec["plain"]],
        ),
        out_shape=[shape, shape],
        compiler_params=pltpu.CompilerParams(vmem_limit_bytes=VMEM_BYTES),
        name="early",
        cost_estimate=lasting(4.5),
    )(place, q_near, k_own, values, k2, *v2, joined)


def late_part(group, per_group, skip, count, place, q_near, k1, v1, steps, joined, early, scale):
    _, rows, dh = q_near.shape
    length = early[0].shape[1]
    spec = cross_specs(group, per_group, length, rows, dh, skip)
    names = ["all", "part", "half_values", "half_values", "step", "step", "plain", "plain"]
    return pl.pallas_call(
        functools.partial(late_kernel, scale=scale),
        grid_spec=pltpu.PrefetchScalarGridSpec(
            num_scalar_prefetch=1,
            grid=(count,),
            in_specs=[spec[name] for name in names],
            out_specs=pl.BlockSpec((1, rows, dh), lambda h, p: (h, 0, 0)),
        ),
        out_shape=jax.ShapeDtypeStruct((count, rows, dh), jnp.float32),
        compiler_params=pltpu.CompilerParams(vmem_limit_bytes=VMEM_BYTES),
        name="late",
        cost_estimate=lasting(2 * count),
    )(place, q_near, k1, *v1, steps, joined, *early)


def own_part(group, per_group, place, q_own, k1, v1, near_steps, joined, od, ld, scale):
    length = od.shape[1]
    _, rows, dh = q_own.shape
    spec = cross_specs(group, per_group, length, rows, dh)
    names = ["all", "part", "half_values", "half_values", "step", "step", "all_plain", "all_plain"]
    shape = jax.ShapeDtypeStruct((per_group, length, dh), jnp.float32)
    return pl.pallas_call(
        functools.partial(own_kernel, scale=scale),
        grid_spec=pltpu.PrefetchScalarGridSpec(
            num_scalar_prefetch=1,
            grid=(per_group,),
            in_specs=[spec[name] for name in names],
            out_specs=[spec["plain"], spec["plain"]],
        ),
        out_shape=[shape, shape],
        compiler_params=pltpu.CompilerParams(vmem_limit_bytes=VMEM_BYTES),
        name="own",
        cost_estimate=lasting(4.5),
    )(place, q_own, k1, *v1, near_steps, joined, od, ld)


def merge_kernel(core_ref, o_ref, lse_ref, msg_ref, keep_ref, send_ref):
    length, dh = o_ref.shape[1:]
    share = keep_ref.shape[0]
    parts = []
    for i in range(length // PIECE):
        span = slice(i * PIECE, (i + 1) * PIECE)
        lse = lse_ref[0, span, :]
        lse_p = columns_of(msg_ref[0, length + i : length + i + 1, :])
        peak = jnp.maximum(lse, lse_p)
        w, w_p = jnp.exp2(lse - peak), jnp.exp2(lse_p - peak)
        parts.append((o_ref[0, span, :] * w + msg_ref[0, span, :] * w_p) / (w + w_p))
    whole = jnp.concatenate(parts, axis=0)
    first = core_ref[0] == 0
    low, high = whole[:share], whole[share:]
    keep_ref[...] = jnp.where(first, low, high)
    send_ref[...] = jnp.where(first, high, low)


def merge(core, o, lse, msg, skip):
    _, length, dh = o.shape
    count = msg.shape[0]
    share = length // 2
    head = pl.BlockSpec((1, length, dh), lambda h, c: (skip + h, 0, 0))
    out = pl.BlockSpec((share, dh), lambda h, c: (0, h))
    shape = jax.ShapeDtypeStruct((share, count * dh), jnp.float32)
    return pl.pallas_call(
        merge_kernel,
        grid_spec=pltpu.PrefetchScalarGridSpec(
            num_scalar_prefetch=1,
            grid=(count,),
            in_specs=[head, head, pl.BlockSpec((1,) + msg.shape[1:], lambda h, c: (h, 0, 0))],
            out_specs=[out, out],
        ),
        out_shape=[shape, shape],
        compiler_params=pltpu.CompilerParams(vmem_limit_bytes=VMEM_BYTES),
        name="merge",
        cost_estimate=lasting(2.2),
    )(core, o, lse, msg)


def halves_kernel(own_ref, other_ref, *out_refs):
    for ref, (high, low) in zip((own_ref, other_ref), (out_refs[:2], out_refs[2:])):
        high[pl.program_id(0)], low[pl.program_id(0)] = split(ref[...])


def weight_halves(w_own, w_other):
    depth, width = w_own.shape
    tile = min(width, TILE)
    spec = pl.BlockSpec((depth, tile), lambda n: (0, n))
    kept = pl.BlockSpec(memory_space=pltpu.VMEM)
    return pl.pallas_call(
        halves_kernel,
        grid=(width // tile,),
        in_specs=[spec] * 2,
        out_specs=[kept] * 4,
        out_shape=[pltpu.VMEM((width // tile, depth, tile), jnp.bfloat16)] * 4,
        compiler_params=pltpu.CompilerParams(vmem_limit_bytes=VMEM_BYTES),
        name="weight_halves",
        cost_estimate=lasting(7),
    )(w_own, w_other)


def project_kernel(*refs):
    *a_refs, own_high, own_low, other_high, other_low, out_ref = refs
    half = len(a_refs) // 2
    parts = []
    for part, high, low in ((a_refs[:half], own_high, own_low), (a_refs[half:], other_high, other_low)):
        a_high, a_low = split(jnp.concatenate([r[...] for r in part], axis=1))
        stacked = scored(jnp.concatenate([a_high, a_low], axis=0), high[pl.program_id(0)])
        rows = a_high.shape[0]
        parts.append(stacked[:rows] + (stacked[rows:] + scored(a_high, low[pl.program_id(0)])))
    out_ref[...] = parts[0] + parts[1]


def project(kept, received, weights):
    share = kept[0].shape[0]
    tiles, depth, tile = weights[0].shape
    width = tiles * tile
    a_spec = [pl.BlockSpec(a.shape, lambda n: (0, 0)) for a in kept + received]
    w_spec = pl.BlockSpec(memory_space=pltpu.VMEM)
    return pl.pallas_call(
        project_kernel,
        grid=(tiles,),
        in_specs=a_spec + [w_spec] * 4,
        out_specs=pl.BlockSpec((share, tile), lambda n: (0, n)),
        out_shape=jax.ShapeDtypeStruct((share, width), jnp.float32),
        compiler_params=pltpu.CompilerParams(vmem_limit_bytes=VMEM_BYTES),
        name="project",
        cost_estimate=lasting(7.5),
    )(*kept, *received, *weights)


def onward(value, steps):
    count = lax.axis_size("ctx")
    return lax.ppermute(value, "ctx", [(i, (i + steps) % count) for i in range(count)])


def exchanged(value, axis, bit):
    return lax.ppermute(value, axis, [(i, i ^ bit) for i in range(lax.axis_size(axis))])


def after(value, *others):
    return lax.optimization_barrier((value,) + others)[0]


def shards(queries, keys, values, transitions, betas, documents, out_weight):
    heads, length = betas.shape
    dh = queries.shape[1] // heads
    assert length == BLOCK_TOKENS and lax.axis_size("ctx") % 4 == 0 and lax.axis_size("head") == 2
    per_group = heads // GROUPS
    groups = range(GROUPS)
    scale = math.log2(math.e) / math.sqrt(dh)
    index = lax.axis_index("ctx").astype(jnp.int32)
    place = index.reshape(1)
    core = lax.axis_index("head").astype(jnp.int32).reshape(1)
    far_side = lax.rem(index, 4) >= 2
    v_first, v_last = values[: length // 2], values[length // 2 :]

    def chosen(block, behind):
        return jnp.where(far_side, behind, block)

    v2_first = onward(v_first, 4)
    w_other = exchanged(out_weight, "head", 1)
    prepared = prepare(queries, keys, values, transitions, betas, documents, scale)
    q_msg, k_msg, steps, od, ld, v2_first, w_other = lax.optimization_barrier((*prepared, v2_first, w_other))
    own_k = [k_msg[g * per_group : (g + 1) * per_group] for g in groups]
    near_steps = exchanged(steps, "ctx", 1)
    v1_first = exchanged(chosen(v_first, v2_first), "ctx", 2)
    v2_last = onward(after(v_last, steps), 4)
    q_near = exchanged(after(q_msg, near_steps), "ctx", 1)
    joined = joined_steps(place, steps, near_steps)
    joined = onward(joined, 2)
    source = chosen(v_last, v2_last)
    v1_last = exchanged(source, "ctx", 2)
    k2 = [onward(after(own_k[0], source), 4)]
    k2 += [onward(after(block, joined, source), 4) for block in own_k[1:]]
    weights = weight_halves(out_weight, after(w_other, joined, source))
    sources = [chosen(after(own_k[0], v1_first, v1_last), k2[0])]
    v1, v2 = (v1_first, v1_last), (v2_first, v2_last)
    early = []
    for g in groups:
        if g:
            sources.append(chosen(after(own_k[g], early[-1][0]), k2[g]))
        ready = after(place, sources[g], *weights)
        early.append(early_part(g, per_group, ready, q_near, k_msg, values, k2[g], v2, joined, scale))
    k1 = [exchanged(source, "ctx", 2) for source in sources]
    kept, received = [], []
    for g in groups:
        count = per_group if g < GROUPS - 1 else 1
        spans = range(0, per_group, count)
        messages = [
            late_part(g, per_group, skip, count, place, q_near, k1[g], v1, steps, joined, early[g], scale)
            for skip in spans
        ]
        out, lse = own_part(g, per_group, place, q_msg, k1[g], v1, near_steps, joined, od, ld, scale)
        for skip, msg in zip(spans, messages):
            keep, send = merge(core, out, lse, exchanged(msg, "ctx", 1), skip)
            kept.append(keep)
            received.append(exchanged(send, "head", 1))
    return project(kept, received, weights)


def solution(mesh):
    return jax.shard_map(
        shards,
        mesh=mesh,
        in_specs=(
            P("ctx", "head"),
            P("ctx", "head"),
            P("ctx", "head"),
            P("ctx", "head"),
            P("head", "ctx"),
            P("ctx"),
            P("head", None),
        ),
        out_specs=P(("ctx", "head"), None),
        check_vma=False,
    )
```

```python
import functools
import math

import jax
import jax.numpy as jnp
from jax import lax
from jax.experimental import pallas as pl
from jax.experimental.pallas import tpu as pltpu
from jax.sharding import PartitionSpec as P

BLOCK_TOKENS = 512
PIECE = 128
SEED = 16
BATCH = 2
ROWS = 512
TILE = 512
GROUPS = 2
FAR = -1e30
VMEM_BYTES = 36 * 2**20
PREPARE_BYTES = 60 * 2**20
COST = 1.15e9


def lasting(microseconds):
    return pl.CostEstimate(flops=int(microseconds * COST), bytes_accessed=1000, transcendentals=0)


def split(value):
    high = value.astype(jnp.bfloat16)
    return high, (value - high.astype(jnp.float32)).astype(jnp.bfloat16)


def product(left, right, left_dim, right_dim):
    left_high, left_low = split(left)
    right_high, right_low = split(right)
    return lax.dot_general(
        jnp.concatenate([left_high, left_low, left_high], axis=left_dim),
        jnp.concatenate([right_high, right_high, right_low], axis=right_dim),
        (((left_dim,), (right_dim,)), ((), ())),
        preferred_element_type=jnp.float32,
    )


def mm(left, right):
    return product(left, right, 1, 0)


def mm_nt(left, right):
    return product(left, right, 1, 1)


def mm_tn(left, right):
    return product(left, right, 0, 0)


def columns_of(row):
    parts = [
        jnp.broadcast_to(row[:, i : i + PIECE], (PIECE, PIECE)).T
        for i in range(0, row.shape[1], PIECE)
    ]
    return jnp.concatenate(parts, axis=0) if len(parts) > 1 else parts[0]


def unit_lower_inverses(stricts):
    order = stricts[0].shape[0]
    blocks = order // SEED
    rows = lax.broadcasted_iota(jnp.int32, (order, order), 0)
    cols = lax.broadcasted_iota(jnp.int32, (order, order), 1)
    diagonal = rows // SEED == cols // SEED
    packed = []
    for strict in stricts:
        kept = jnp.where(diagonal, strict, 0.0)
        total = kept[:SEED]
        for block in range(1, blocks):
            total = total + kept[block * SEED : (block + 1) * SEED]
        packed.append(total)
    packed = jnp.concatenate(packed, axis=0)
    lane = lax.broadcasted_iota(jnp.int32, packed.shape, 1)
    row = lax.broadcasted_iota(jnp.int32, packed.shape, 0)
    shape = (len(stricts), SEED, order)
    inverse = jnp.where(lane % SEED == row % SEED, 1.0, 0.0).reshape(shape)
    first = lane - lane % SEED
    for k in range(SEED - 1):
        column = jnp.take_along_axis(packed, first + k, axis=1, mode="promise_in_bounds")
        inverse = inverse - column.reshape(shape) * inverse[:, k : k + 1, :]
    inverses = [
        jnp.where(diagonal, jnp.concatenate([inverse[i]] * blocks, axis=0), 0.0)
        for i in range(len(stricts))
    ]
    size = SEED
    while size < order:
        below = (rows // size == cols // size + 1) & (rows // (2 * size) == cols // (2 * size))
        right = [mm(jnp.where(below, s, 0.0), x) for s, x in zip(stricts, inverses)]
        inverses = [x - mm(x, r) for x, r in zip(inverses, right)]
        size *= 2
    return inverses


def stacked_values(values):
    return jnp.concatenate(split(values), axis=1)


def softmax_part(scores, stacked):
    rows, dh = scores.shape[0], stacked.shape[1] // 2
    peak = jnp.max(scores, axis=-1, keepdims=True)
    weights = jnp.exp2(scores - peak)
    total = jnp.sum(weights, axis=-1, keepdims=True)
    summed = lax.dot_general(
        jnp.concatenate(split(weights), axis=0), stacked, (((1,), (0,)), ((), ())),
        preferred_element_type=jnp.float32,
    )
    summed = summed[:rows] + summed[rows:]
    return (summed[:, :dh] + summed[:, dh:]) / total, peak + jnp.log2(total)


def stacked_keys(keys):
    high, low = split(keys)
    return jnp.concatenate([high, high, low], axis=1).T


def stacked_queries(queries):
    high, low = split(queries)
    return jnp.concatenate([high, low, high], axis=1)


def scored(queries, keys):
    return lax.dot_general(queries, keys, (((1,), (0,)), ((), ())), preferred_element_type=jnp.float32)


def prepare_kernel(q_ref, k_ref, v_ref, w_ref, beta_ref, doc_ref, qo_ref, ko_ref, st_ref, o_ref, lse_ref, *, scale):
    batch, dh, _ = st_ref.shape
    length = q_ref.shape[0]
    pieces = length // PIECE
    rows = lax.broadcasted_iota(jnp.int32, (PIECE, PIECE), 0)
    cols = lax.broadcasted_iota(jnp.int32, (PIECE, PIECE), 1)
    identity = jnp.where(rows == cols, 1.0, 0.0)
    spans = [slice(i * PIECE, (i + 1) * PIECE) for i in range(pieces)]
    heads = [slice(h * dh, (h + 1) * dh) for h in range(batch)]
    where = [(head, span) for head in heads for span in spans]
    directions = [w_ref[span, head] for head, span in where]
    units = [w * lax.rsqrt(jnp.sum(w * w, axis=-1, keepdims=True) + 1e-06) for w in directions]
    first = pl.program_id(0) * batch
    beta_rows = [beta_ref[pl.ds(first + h, 1), :] for h in range(batch)]
    betas = [columns_of(row[:, span]) for row in beta_rows for span in spans]
    grams = [
        mm_nt(jnp.concatenate([t, q_ref[span, head]], axis=0), jnp.concatenate([t, k_ref[span, head]], axis=0))
        for t, (head, span) in zip(units, where)
    ]
    inverses = unit_lower_inverses(
        [jnp.where(rows > cols, beta * g[:PIECE, :PIECE], 0.0) for beta, g in zip(betas, grams)]
    )
    solved = [
        mm(x, jnp.concatenate([jnp.where(rows > cols, beta * g[:PIECE, PIECE:], 0.0), beta * t], axis=1))
        for x, beta, g, t in zip(inverses, betas, grams, units)
    ]
    change = [mm(jnp.where(rows >= cols, g[PIECE:, :PIECE], 0.0), s) for g, s in zip(grams, solved)]
    carried = [mm_tn(s, t) for s, t in zip(solved, units)]

    def by_head(flat):
        return [flat[h * pieces : (h + 1) * pieces] for h in range(batch)]

    own = by_head([g[PIECE:, PIECE:] - c[:, :PIECE] for g, c in zip(grams, change)])
    q_hat = by_head([q_ref[span, head] - c[:, PIECE:] for (head, span), c in zip(where, change)])
    k_hat = by_head([k_ref[span, head] - c[:PIECE] for (head, span), c in zip(where, carried)])
    st = by_head([identity - c[PIECE:] for c in carried])
    tiles = [[[None] * pieces for _ in range(pieces)] for _ in range(batch)]
    for h in range(batch):
        for i in range(pieces):
            tiles[h][i][i] = own[h][i]
    current = [list(q) for q in q_hat]
    suffix = [[None] * pieces for _ in range(batch)]
    for back in range(1, pieces):
        for h in range(batch):
            for i in range(back, pieces):
                tiles[h][i][i - back] = mm_nt(current[h][i], k_hat[h][i - back])
                current[h][i] = mm_nt(current[h][i], st[h][i - back])
            j = pieces - back
            suffix[h][j - 1] = st[h][j] if back == 1 else mm(st[h][j], suffix[h][j])
    for h in range(batch):
        for i in range(pieces):
            qo_ref[h, spans[i], :] = current[h][i]
            ko_ref[h, spans[i], :] = k_hat[h][i] if i == pieces - 1 else mm(k_hat[h][i], suffix[h][i])
        st_ref[h] = mm(st[h][0], suffix[h][0]) if pieces > 1 else st[h][0]
    doc_row = (doc_ref[...].reshape(1, length) + 1).astype(jnp.float32)
    doc_col = columns_of(doc_row)
    doc_lines = [doc_row[:, span] for span in spans]
    doc_lines.append(jnp.zeros((qo_ref.shape[1] - length - pieces, dh), jnp.float32))
    doc_lines = jnp.concatenate(doc_lines, axis=0)
    for h in range(batch):
        qo_ref[h, length:, :] = doc_lines
        ko_ref[h, length:, :] = doc_lines
    stacked = [stacked_values(v_ref[:, head]) for head in heads]
    for i in range(pieces):
        for h in range(batch):
            masked = []
            for j in range(i + 1):
                same = doc_col[spans[i]] == doc_row[:, spans[j]]
                if i == j:
                    same = same & (rows >= cols)
                masked.append(jnp.where(same, tiles[h][i][j] * scale, FAR))
            out, lse = softmax_part(
                jnp.concatenate(masked, axis=1) if i else masked[0], stacked[h][: (i + 1) * PIECE]
            )
            o_ref[h, spans[i], :] = out
            lse_ref[h, spans[i], :] = jnp.broadcast_to(lse, (PIECE, PIECE))


def message_rows(length):
    return length + (length // PIECE + 7) // 8 * 8


def prepare(queries, keys, values, transitions, betas, documents, scale):
    length = queries.shape[0]
    heads = betas.shape[0]
    dh = queries.shape[1] // heads
    rows = message_rows(length)
    column = pl.BlockSpec((length, BATCH * dh), lambda h: (0, h))
    head = pl.BlockSpec((BATCH, length, dh), lambda h: (h, 0, 0))
    message = pl.BlockSpec((BATCH, rows, dh), lambda h: (h, 0, 0))
    f32 = jnp.float32
    return pl.pallas_call(
        functools.partial(prepare_kernel, scale=scale),
        grid=(heads // BATCH,),
        in_specs=[column] * 4
        + [
            pl.BlockSpec((heads, length), lambda h: (0, 0)),
            pl.BlockSpec((length,), lambda h: (0,)),
        ],
        out_specs=[message, message, pl.BlockSpec((BATCH, dh, dh), lambda h: (h, 0, 0)), head, head],
        out_shape=[
            jax.ShapeDtypeStruct((heads, rows, dh), f32),
            jax.ShapeDtypeStruct((heads, rows, dh), f32),
            jax.ShapeDtypeStruct((heads, dh, dh), f32),
            jax.ShapeDtypeStruct((heads, length, dh), f32),
            jax.ShapeDtypeStruct((heads, length, dh), f32),
        ],
        compiler_params=pltpu.CompilerParams(vmem_limit_bytes=PREPARE_BYTES),
        name="prepare",
        cost_estimate=lasting(13),
    )(queries, keys, values, transitions, betas, documents)


def steps_kernel(place_ref, own_ref, near_ref, out_ref):
    even = lax.rem(place_ref[0], 2) == 0
    for h in range(own_ref.shape[0]):
        near = near_ref[h]
        out_ref[h] = jnp.where(even, near, mm(near, own_ref[h]))


def joined_steps(place, own, near):
    whole = pl.BlockSpec(own.shape, lambda i, p: (0, 0, 0))
    return pl.pallas_call(
        steps_kernel,
        grid_spec=pltpu.PrefetchScalarGridSpec(
            num_scalar_prefetch=1, grid=(1,), in_specs=[whole, whole], out_specs=whole
        ),
        out_shape=jax.ShapeDtypeStruct(own.shape, jnp.float32),
        compiler_params=pltpu.CompilerParams(vmem_limit_bytes=VMEM_BYTES),
        name="joined_steps",
        cost_estimate=lasting(2),
    )(place, own, near)


def doc_line(ref, length, valid):
    line = jnp.concatenate([ref[0, length + i : length + i + 1, :] for i in range(length // PIECE)], axis=1)
    return jnp.where(valid, line, 0.0)


def masked(scores, col, row):
    wide = jnp.concatenate([col] * (scores.shape[1] // PIECE), axis=1)
    return jnp.where(wide == row, scores, FAR)


def attended_part(query, keys, values, docs, col):
    parts = []
    for start in range(0, query.shape[0], ROWS):
        span = slice(start, start + ROWS)
        parts.append((span, *softmax_part(masked(scored(query[span], keys), col[span], docs), values)))
    return parts


def joined_parts(out, lse, other, other_lse):
    peak = jnp.maximum(lse, other_lse)
    w, w_other = jnp.exp2(lse - peak), jnp.exp2(other_lse - peak)
    total = w + w_other
    return (out * w + other * w_other) / total, peak + jnp.log2(total)


def early_kernel(place_ref, qp_ref, ko_ref, vo_ref, k2_ref, v2a_ref, v2b_ref, u_ref, out_ref, lse_ref, *, scale):
    length, dh = vo_ref.shape
    place = place_ref[0]
    pick = lambda a, b: jnp.where(lax.rem(place, 2) == 0, a, b)
    docs = pick(doc_line(ko_ref, length, True), doc_line(k2_ref, length, place >= 4))
    keys = stacked_keys(pick(ko_ref[0, :length, :], mm(k2_ref[0, :length, :], u_ref[0])))
    values = stacked_values(
        pick(vo_ref[...], jnp.concatenate([v2a_ref[...], v2b_ref[...]], axis=0))
    )
    query = stacked_queries(qp_ref[0, :length, :] * scale)
    col = columns_of(doc_line(qp_ref, length, True))
    for span, out, lse in attended_part(query, keys, values, docs, col):
        out_ref[0, span, :] = out
        lse_ref[0, span, :] = jnp.broadcast_to(lse, (ROWS, dh))


def late_kernel(place_ref, qp_ref, k1_ref, v1a_ref, v1b_ref, s_ref, u_ref, oe_ref, le_ref, msg_ref, *, scale):
    length = oe_ref.shape[1]
    place = place_ref[0]
    pick = lambda a, b: jnp.where(lax.rem(place, 2) == 0, a, b)
    docs = doc_line(k1_ref, length, place >= 2)
    k1 = k1_ref[0, :length, :]
    keys = stacked_keys(pick(mm(k1, u_ref[0]), k1))
    values = stacked_values(jnp.concatenate([v1a_ref[...], v1b_ref[...]], axis=0))
    query = qp_ref[0, :length, :] * scale
    query = stacked_queries(pick(mm_nt(query, s_ref[0]), query))
    col = columns_of(doc_line(qp_ref, length, True))
    for span, out, lse in attended_part(query, keys, values, docs, col):
        out, lse = joined_parts(out, lse, oe_ref[0, span, :], le_ref[0, span, :])
        msg_ref[0, span, :] = out
        for i in range(0, ROWS, PIECE):
            line = length + (span.start + i) // PIECE
            msg_ref[0, line : line + 1, :] = lse[i : i + PIECE].T[:1]
    first = length + length // PIECE
    msg_ref[0, first:, :] = jnp.zeros((msg_ref.shape[1] - first, msg_ref.shape[2]), jnp.float32)


def own_kernel(place_ref, qo_ref, k1_ref, v1a_ref, v1b_ref, s_ref, u_ref, od_ref, ld_ref, out_ref, lse_ref, *, scale):
    length = od_ref.shape[1]
    place = place_ref[0]
    even = lax.rem(place, 2) == 0
    pick = lambda a, b: jnp.where(even, a, b)
    docs = doc_line(k1_ref, length, place >= 2)
    k1 = k1_ref[0, :length, :]
    keys = stacked_keys(pick(mm(k1, u_ref[0]), k1))
    values = stacked_values(jnp.concatenate([v1a_ref[...], v1b_ref[...]], axis=0))
    query = qo_ref[0, :length, :] * scale
    query = stacked_queries(pick(query, mm_nt(query, s_ref[0])))
    col = columns_of(doc_line(qo_ref, length, True))
    for span, out, lse in attended_part(query, keys, values, docs, col):
        out, lse = joined_parts(out, lse, od_ref[0, span, :], ld_ref[0, span, :])
        out_ref[0, span, :] = out
        lse_ref[0, span, :] = lse


def cross_specs(group, per_group, length, rows, dh, skip=0):
    return {
        "all": pl.BlockSpec((1, rows, dh), lambda h, p: (group * per_group + skip + h, 0, 0)),
        "part": pl.BlockSpec((1, rows, dh), lambda h, p: (skip + h, 0, 0)),
        "all_values": pl.BlockSpec((length, dh), lambda h, p: (0, group * per_group + skip + h)),
        "half_values": pl.BlockSpec((length // 2, dh), lambda h, p: (0, group * per_group + skip + h)),
        "step": pl.BlockSpec((1, dh, dh), lambda h, p: (group * per_group + skip + h, 0, 0)),
        "all_plain": pl.BlockSpec((1, length, dh), lambda h, p: (group * per_group + skip + h, 0, 0)),
        "plain": pl.BlockSpec((1, length, dh), lambda h, p: (skip + h, 0, 0)),
    }


def early_part(group, per_group, place, q_near, k_own, values, k2, v2, joined, scale):
    length = values.shape[0]
    _, rows, dh = q_near.shape
    spec = cross_specs(group, per_group, length, rows, dh)
    names = ["all", "all", "all_values", "part", "half_values", "half_values", "step"]
    shape = jax.ShapeDtypeStruct((per_group, length, dh), jnp.float32)
    return pl.pallas_call(
        functools.partial(early_kernel, scale=scale),
        grid_spec=pltpu.PrefetchScalarGridSpec(
            num_scalar_prefetch=1,
            grid=(per_group,),
            in_specs=[spec[name] for name in names],
            out_specs=[spec["plain"], spec["plain"]],
        ),
        out_shape=[shape, shape],
        compiler_params=pltpu.CompilerParams(vmem_limit_bytes=VMEM_BYTES),
        name="early",
        cost_estimate=lasting(4.5),
    )(place, q_near, k_own, values, k2, *v2, joined)


def late_part(group, per_group, skip, count, place, q_near, k1, v1, steps, joined, early, scale):
    _, rows, dh = q_near.shape
    length = early[0].shape[1]
    spec = cross_specs(group, per_group, length, rows, dh, skip)
    names = ["all", "part", "half_values", "half_values", "step", "step", "plain", "plain"]
    return pl.pallas_call(
        functools.partial(late_kernel, scale=scale),
        grid_spec=pltpu.PrefetchScalarGridSpec(
            num_scalar_prefetch=1,
            grid=(count,),
            in_specs=[spec[name] for name in names],
            out_specs=pl.BlockSpec((1, rows, dh), lambda h, p: (h, 0, 0)),
        ),
        out_shape=jax.ShapeDtypeStruct((count, rows, dh), jnp.float32),
        compiler_params=pltpu.CompilerParams(vmem_limit_bytes=VMEM_BYTES),
        name="late",
        cost_estimate=lasting(2 * count),
    )(place, q_near, k1, *v1, steps, joined, *early)


def own_part(group, per_group, place, q_own, k1, v1, near_steps, joined, od, ld, scale):
    length = od.shape[1]
    _, rows, dh = q_own.shape
    spec = cross_specs(group, per_group, length, rows, dh)
    names = ["all", "part", "half_values", "half_values", "step", "step", "all_plain", "all_plain"]
    shape = jax.ShapeDtypeStruct((per_group, length, dh), jnp.float32)
    return pl.pallas_call(
        functools.partial(own_kernel, scale=scale),
        grid_spec=pltpu.PrefetchScalarGridSpec(
            num_scalar_prefetch=1,
            grid=(per_group,),
            in_specs=[spec[name] for name in names],
            out_specs=[spec["plain"], spec["plain"]],
        ),
        out_shape=[shape, shape],
        compiler_params=pltpu.CompilerParams(vmem_limit_bytes=VMEM_BYTES),
        name="own",
        cost_estimate=lasting(4.5),
    )(place, q_own, k1, *v1, near_steps, joined, od, ld)


def merge_kernel(core_ref, o_ref, lse_ref, msg_ref, keep_ref, send_ref):
    length, dh = o_ref.shape[1:]
    share = keep_ref.shape[0]
    parts = []
    for i in range(length // PIECE):
        span = slice(i * PIECE, (i + 1) * PIECE)
        lse = lse_ref[0, span, :]
        lse_p = columns_of(msg_ref[0, length + i : length + i + 1, :])
        peak = jnp.maximum(lse, lse_p)
        w, w_p = jnp.exp2(lse - peak), jnp.exp2(lse_p - peak)
        parts.append((o_ref[0, span, :] * w + msg_ref[0, span, :] * w_p) / (w + w_p))
    whole = jnp.concatenate(parts, axis=0)
    first = core_ref[0] == 0
    low, high = whole[:share], whole[share:]
    keep_ref[...] = jnp.where(first, low, high)
    send_ref[...] = jnp.where(first, high, low)


def merge(core, o, lse, msg, skip):
    _, length, dh = o.shape
    count = msg.shape[0]
    share = length // 2
    head = pl.BlockSpec((1, length, dh), lambda h, c: (skip + h, 0, 0))
    out = pl.BlockSpec((share, dh), lambda h, c: (0, h))
    shape = jax.ShapeDtypeStruct((share, count * dh), jnp.float32)
    return pl.pallas_call(
        merge_kernel,
        grid_spec=pltpu.PrefetchScalarGridSpec(
            num_scalar_prefetch=1,
            grid=(count,),
            in_specs=[head, head, pl.BlockSpec((1,) + msg.shape[1:], lambda h, c: (h, 0, 0))],
            out_specs=[out, out],
        ),
        out_shape=[shape, shape],
        compiler_params=pltpu.CompilerParams(vmem_limit_bytes=VMEM_BYTES),
        name="merge",
        cost_estimate=lasting(2.2),
    )(core, o, lse, msg)


def halves_kernel(own_ref, other_ref, *out_refs):
    for ref, (high, low) in zip((own_ref, other_ref), (out_refs[:2], out_refs[2:])):
        high[pl.program_id(0)], low[pl.program_id(0)] = split(ref[...])


def weight_halves(w_own, w_other):
    depth, width = w_own.shape
    tile = min(width, TILE)
    spec = pl.BlockSpec((depth, tile), lambda n: (0, n))
    kept = pl.BlockSpec(memory_space=pltpu.VMEM)
    return pl.pallas_call(
        halves_kernel,
        grid=(width // tile,),
        in_specs=[spec] * 2,
        out_specs=[kept] * 4,
        out_shape=[pltpu.VMEM((width // tile, depth, tile), jnp.bfloat16)] * 4,
        compiler_params=pltpu.CompilerParams(vmem_limit_bytes=VMEM_BYTES),
        name="weight_halves",
        cost_estimate=lasting(7),
    )(w_own, w_other)


def project_kernel(*refs):
    *a_refs, own_high, own_low, other_high, other_low, out_ref = refs
    half = len(a_refs) // 2
    parts = []
    for part, high, low in ((a_refs[:half], own_high, own_low), (a_refs[half:], other_high, other_low)):
        a_high, a_low = split(jnp.concatenate([r[...] for r in part], axis=1))
        stacked = scored(jnp.concatenate([a_high, a_low], axis=0), high[pl.program_id(0)])
        rows = a_high.shape[0]
        parts.append(stacked[:rows] + (stacked[rows:] + scored(a_high, low[pl.program_id(0)])))
    out_ref[...] = parts[0] + parts[1]


def project(kept, received, weights):
    share = kept[0].shape[0]
    tiles, depth, tile = weights[0].shape
    width = tiles * tile
    a_spec = [pl.BlockSpec(a.shape, lambda n: (0, 0)) for a in kept + received]
    w_spec = pl.BlockSpec(memory_space=pltpu.VMEM)
    return pl.pallas_call(
        project_kernel,
        grid=(tiles,),
        in_specs=a_spec + [w_spec] * 4,
        out_specs=pl.BlockSpec((share, tile), lambda n: (0, n)),
        out_shape=jax.ShapeDtypeStruct((share, width), jnp.float32),
        compiler_params=pltpu.CompilerParams(vmem_limit_bytes=VMEM_BYTES),
        name="project",
        cost_estimate=lasting(7.5),
    )(*kept, *received, *weights)


def onward(value, steps):
    count = lax.axis_size("ctx")
    return lax.ppermute(value, "ctx", [(i, (i + steps) % count) for i in range(count)])


def exchanged(value, axis, bit):
    return lax.ppermute(value, axis, [(i, i ^ bit) for i in range(lax.axis_size(axis))])


def after(value, *others):
    return lax.optimization_barrier((value,) + others)[0]


def shards(queries, keys, values, transitions, betas, documents, out_weight):
    heads, length = betas.shape
    dh = queries.shape[1] // heads
    assert length == BLOCK_TOKENS and lax.axis_size("ctx") % 4 == 0 and lax.axis_size("head") == 2
    per_group = heads // GROUPS
    groups = range(GROUPS)
    scale = math.log2(math.e) / math.sqrt(dh)
    index = lax.axis_index("ctx").astype(jnp.int32)
    place = index.reshape(1)
    core = lax.axis_index("head").astype(jnp.int32).reshape(1)
    far_side = lax.rem(index, 4) >= 2
    v_first, v_last = values[: length // 2], values[length // 2 :]

    def chosen(block, behind):
        return jnp.where(far_side, behind, block)

    v2_first = onward(v_first, 4)
    w_other = exchanged(out_weight, "head", 1)
    prepared = prepare(queries, keys, values, transitions, betas, documents, scale)
    q_msg, k_msg, steps, od, ld, v2_first, w_other = lax.optimization_barrier((*prepared, v2_first, w_other))
    own_k = [k_msg[g * per_group : (g + 1) * per_group] for g in groups]
    near_steps = exchanged(steps, "ctx", 1)
    v1_first = exchanged(chosen(v_first, v2_first), "ctx", 2)
    v2_last = onward(after(v_last, steps), 4)
    q_near = exchanged(after(q_msg, near_steps), "ctx", 1)
    joined = joined_steps(place, steps, near_steps)
    joined = onward(joined, 2)
    source = chosen(v_last, v2_last)
    v1_last = exchanged(source, "ctx", 2)
    k2 = [onward(after(own_k[0], source), 4)]
    k2 += [onward(after(block, joined, source), 4) for block in own_k[1:]]
    weights = weight_halves(out_weight, after(w_other, joined, source))
    sources = [chosen(after(own_k[0], v1_first, v1_last), k2[0])]
    v1, v2 = (v1_first, v1_last), (v2_first, v2_last)
    early = []
    for g in groups:
        if g:
            sources.append(chosen(after(own_k[g], early[-1][0]), k2[g]))
        ready = after(place, sources[g], *weights)
        early.append(early_part(g, per_group, ready, q_near, k_msg, values, k2[g], v2, joined, scale))
    k1 = [exchanged(source, "ctx", 2) for source in sources]
    kept, received = [], []
    for g in groups:
        count = per_group if g < GROUPS - 1 else 1
        spans = range(0, per_group, count)
        messages = [
            late_part(g, per_group, skip, count, place, q_near, k1[g], v1, steps, joined, early[g], scale)
            for skip in spans
        ]
        out, lse = own_part(g, per_group, place, q_msg, k1[g], v1, near_steps, joined, od, ld, scale)
        for skip, msg in zip(spans, messages):
            keep, send = merge(core, out, lse, exchanged(msg, "ctx", 1), skip)
            kept.append(keep)
            received.append(exchanged(send, "head", 1))
    return project(kept, received, weights)


def solution(mesh):
    return jax.shard_map(
        shards,
        mesh=mesh,
        in_specs=(
            P("ctx", "head"),
            P("ctx", "head"),
            P("ctx", "head"),
            P("ctx", "head"),
            P("head", "ctx"),
            P("ctx"),
            P("head", None),
        ),
        out_specs=P(("ctx", "head"), None),
        check_vma=False,
    )
```
